32 devices in a mesh: dp: 4 (over x, core), expert: 8 (over z, y).
Axes of the slice: x: 2, y: 2, z: 4, core: 2. Of those that a mesh axis runs over, the one named last changes fastest.
Arguments:
- embeds: bfloat16 [8192, 1152], P(('dp', 'expert')), may hold values from -6 to 6
- trunk_gain: float32 [1152], replicated, may hold values from 0.5 to 1.5
- trunk_weight: bfloat16 [1152, 1152], replicated, may hold values from -0.1875 to 0.1875
- w_gate: bfloat16 [32, 1152, 1024], P(('dp', 'expert')), may hold values from -0.1875 to 0.1875
- w_up: bfloat16 [32, 1152, 1024], P(('dp', 'expert')), may hold values from -0.1875 to 0.1875
- w_down: bfloat16 [32, 1024, 1152], P(('dp', 'expert')), may hold values from -0.1875 to 0.1875
- tags: int32 [8192], P(('dp', 'expert')), may hold values from 0 to 31, as said below
- plan: int32 [32], replicated, may hold values from 0 to 31, as said below
- helper: int32 [8192], P(('dp', 'expert')), may hold values from 0 to 31, as said below
- cotangent: bfloat16 [8192, 1152], P(('dp', 'expert')), may hold values from -0.59765625 to 0.59765625
Outputs:
- grad_gate: bfloat16 [32, 1152, 1024], P(('dp', 'expert'))
- grad_up: bfloat16 [32, 1152, 1024], P(('dp', 'expert'))
- grad_down: bfloat16 [32, 1024, 1152], P(('dp', 'expert'))
- grad_trunk: float32 [1152, 1152], P(('dp', 'expert'))
The draws below stay inside these ranges and needn't reach their ends.
Inputs may be any that keep to these rules, and one draw needn't show every extreme that they name: Each token's helper equals its tag, except for tokens tagged with the expert plan[0], which may go to any device. Each device sends exactly 8 tokens to every device (numbered in the order dp then expert). Every device other than device plan[0] receives exactly 8 tokens tagged plan[0]; device plan[0] receives only tokens tagged plan[0]. `tags`: see helper. A permutation of the 32 experts; only plan[0] is served by helpers.
All inputs are finite; a program needn't handle non-finite values.
Results may differ from the reference program's by a relative error of at most 0.003.
The reference program's roundings to bfloat16 on the way count: a program that leaves them out, or rounds other values in their place, can miss the bound.
Values may be sent and summed in bfloat16 or wider, within the bound.
A program may use at most 128 MiB of HBM per device.

```python
import jax
import jax.numpy as jnp
from jax import lax

D = 1152
FF = 1024
TOK_DEV = 256
EXPERTS = 32
TOKENS = 8192
HOT_CAP = 8


def routing_tables(key):
    capacity = TOK_DEV // EXPERTS
    order = jax.random.permutation(jax.random.fold_in(key, 7), EXPERTS).astype(jnp.int32)
    hot_expert = order[0]
    first_keys = jax.random.split(jax.random.fold_in(key, 11), EXPERTS)
    position = jax.vmap(lambda k: jax.random.permutation(k, TOK_DEV))(first_keys).astype(jnp.int32)
    target = position // capacity
    within = position % capacity
    incoming = jnp.arange(EXPERTS, dtype=jnp.int32)[:, None] * capacity + within
    second_keys = jax.random.split(jax.random.fold_in(key, 13), EXPERTS)
    ranking = jax.vmap(lambda k: jax.random.permutation(k, TOK_DEV))(second_keys).astype(jnp.int32)
    chosen = (ranking[target, incoming] < HOT_CAP) & (target != hot_expert)
    tag_table = jnp.where(chosen, hot_expert, target)
    return (tag_table.reshape(-1).astype(jnp.int32), order, target.reshape(-1).astype(jnp.int32))


def draw_tags(key, part):
    return routing_tables(key)[0]


def draw_plan(key, part):
    return routing_tables(key)[1]


def draw_helper(key, part):
    return routing_tables(key)[2]


def shard_levels(own_key, shape, cuts, least, largest):
    loudness = 1.0
    for dim, shards_of in cuts:
        heights = jax.random.uniform(jax.random.fold_in(jax.random.fold_in(own_key, 6), dim), (shards_of,), jnp.float32, least / len(cuts), largest / len(cuts))
        loudness = loudness * jnp.repeat(jnp.exp(heights), shape[dim] // shards_of).reshape((-1,) + (1,) * (len(shape) - 1 - dim))
    return loudness


def bell_draw(key, dims, width, bound, pieces=(), held_as=jnp.bfloat16):
    values = width * jax.random.normal(key, dims, jnp.float32)
    if pieces:
        values = values * shard_levels(key, dims, pieces, -0.22, 0.18)
    return jnp.clip(values, -bound, bound).astype(held_as)


def setup_inputs(seed: int = 0) -> dict:
    splits = jax.random.split(jax.random.key(seed), 11)
    embeds = bell_draw(splits[0], (TOKENS, D), 1.0, 6.0, ((0, 32),))
    trunk_gain = jnp.clip(1.0 + 0.1 * jax.random.normal(splits[1], (D,), jnp.float32), 0.5, 1.5)
    trunk_weight = bell_draw(splits[2], (D, D), D ** -0.5, 0.1875)
    w_gate = bell_draw(splits[3], (EXPERTS, D, FF), D ** -0.5, 0.1875, ((0, 32),))
    w_up = bell_draw(splits[4], (EXPERTS, D, FF), D ** -0.5, 0.1875, ((0, 32),))
    w_down = bell_draw(splits[5], (EXPERTS, FF, D), FF ** -0.5, 0.1875, ((0, 32),))
    tags = draw_tags(jax.random.fold_in(splits[10], 71), 0)
    plan = draw_plan(jax.random.fold_in(splits[10], 71), 0)
    helper = draw_helper(jax.random.fold_in(splits[10], 71), 0)
    cotangent = bell_draw(splits[9], (TOKENS, D), 0.1, 0.59765625, ((0, 32),))
    return {"embeds": embeds, "trunk_gain": trunk_gain, "trunk_weight": trunk_weight, "w_gate": w_gate, "w_up": w_up, "w_down": w_down, "tags": tags, "plan": plan, "helper": helper, "cotangent": cotangent}


def expert_pass(rows, cotan, gate_w, up_w, down_w):
    gate_pre = jnp.dot(rows, gate_w, preferred_element_type=jnp.float32)
    up_pre = jnp.dot(rows, up_w, preferred_element_type=jnp.float32)
    sigma = jax.nn.sigmoid(gate_pre)
    silu_val = gate_pre * sigma
    active = (silu_val * up_pre).astype(jnp.bfloat16)
    d_active = jnp.dot(cotan, down_w.T, preferred_element_type=jnp.float32)
    d_gate = (d_active * up_pre * sigma * (1.0 + gate_pre * (1.0 - sigma))).astype(jnp.bfloat16)
    d_up = (d_active * silu_val).astype(jnp.bfloat16)
    sum_gate = jnp.dot(rows.T, d_gate, preferred_element_type=jnp.float32)
    sum_up = jnp.dot(rows.T, d_up, preferred_element_type=jnp.float32)
    sum_down = jnp.dot(active.T, cotan, preferred_element_type=jnp.float32)
    d_rows = jnp.dot(d_gate, gate_w.T, preferred_element_type=jnp.float32) + jnp.dot(d_up, up_w.T, preferred_element_type=jnp.float32)
    return (sum_gate, sum_up, sum_down, d_rows)

def reference(embeds, trunk_gain, trunk_weight, w_gate, w_up, w_down, tags, plan, helper, cotangent):
    values = embeds.astype(jnp.float32)
    factor = lax.rsqrt(lax.optimization_barrier(jnp.mean(values * values, axis=1, keepdims=True)) + 1e-06)
    normed = (values * factor * trunk_gain).astype(jnp.bfloat16)
    hidden = (values + jnp.dot(normed, trunk_weight, preferred_element_type=jnp.float32)).astype(jnp.bfloat16)
    hot_expert = plan[0]
    by_device = jnp.argsort(helper, stable=True).astype(jnp.int32).reshape(EXPERTS, TOK_DEV)
    foreign = ((tags == hot_expert) & (helper != hot_expert)).astype(jnp.int32)
    hot_index = jnp.argsort(1 - foreign, stable=True).astype(jnp.int32)[:(EXPERTS - 1) * HOT_CAP]
    hot_gate, hot_up, hot_down, hot_drows = expert_pass(hidden[hot_index], cotangent[hot_index], w_gate[hot_expert], w_up[hot_expert], w_down[hot_expert])

    def one_expert(which):
        index = by_device[which]
        rows = hidden[index]
        owned = tags[index] == which
        cotan = jnp.where(owned[:, None], cotangent[index], jnp.zeros_like(cotangent[index]))
        sum_gate, sum_up, sum_down, d_rows = expert_pass(rows, cotan, w_gate[which], w_up[which], w_down[which])
        is_hot = which == hot_expert
        sum_gate = jnp.where(is_hot, sum_gate + hot_gate, sum_gate).astype(jnp.bfloat16)
        sum_up = jnp.where(is_hot, sum_up + hot_up, sum_up).astype(jnp.bfloat16)
        sum_down = jnp.where(is_hot, sum_down + hot_down, sum_down).astype(jnp.bfloat16)
        return (sum_gate, sum_up, sum_down, d_rows)
    grad_gate, grad_up, grad_down, drow_blocks = lax.map(one_expert, jnp.arange(EXPERTS, dtype=jnp.int32))
    dhidden = jnp.zeros((TOKENS, D), jnp.float32)
    dhidden = dhidden.at[by_device.reshape(-1)].add(drow_blocks.reshape(TOKENS, D))
    dhidden = dhidden.at[hot_index].add(hot_drows).astype(jnp.bfloat16)
    grad_trunk = jnp.dot(normed.T, dhidden, preferred_element_type=jnp.float32)
    return (grad_gate, grad_up, grad_down, grad_trunk)
```

```python
import functools
import types

import jax
import jax.numpy as jnp
from jax import lax
from jax.experimental import pallas as pl
from jax.experimental.pallas import tpu as pltpu
from jax.sharding import PartitionSpec as P

LANES = 128
TILE = 16
MESH = pl.DeviceIdType.MESH
MARK, EMB, COT = range(3)
VMEM_BYTES = 45 * 1024 * 1024


def padded(value, multiple):
    return -(-value // multiple) * multiple


def flat_index(experts_axis):
    return lax.axis_index("dp") * experts_axis + lax.axis_index("expert")


def place(flat, experts_axis):
    return (flat // experts_axis, flat % experts_axis)


def flipped(me, bit):
    weight = 1 << bit
    return me + (1 - 2 * ((me // weight) % 2)) * weight


def greet_all(n, experts_axis):
    me = flat_index(experts_axis)
    barrier = pltpu.get_barrier_semaphore()

    def greet(step, carry):
        pl.semaphore_signal(
            barrier,
            inc=1,
            device_id=place(lax.rem(me + step, n), experts_axis),
            device_id_type=MESH,
        )
        return carry

    lax.fori_loop(1, n, greet, 0)
    pl.semaphore_wait(barrier, n - 1)


def greet_bits(bits, experts_axis):
    me = flat_index(experts_axis)
    barrier = pltpu.get_barrier_semaphore()
    for bit in range(bits):
        pl.semaphore_signal(
            barrier, inc=1, device_id=place(flipped(me, bit), experts_axis), device_id_type=MESH
        )
    pl.semaphore_wait(barrier, bits)


def exchange_kernel(n, experts_axis, send_ref, out_ref, send_sem, recv_sem, own_sem):
    me = flat_index(experts_axis)
    greet_all(n, experts_axis)
    own = pltpu.make_async_copy(send_ref.at[me], out_ref.at[me], own_sem)
    own.start()

    def copy_to(step):
        to = lax.rem(me + step, n)
        return pltpu.make_async_remote_copy(
            src_ref=send_ref.at[to],
            dst_ref=out_ref.at[me],
            send_sem=send_sem.at[to],
            recv_sem=recv_sem.at[me],
            device_id=place(to, experts_axis),
            device_id_type=MESH,
        )

    def copy_from(step):
        source = lax.rem(me + step, n)
        return pltpu.make_async_remote_copy(
            src_ref=send_ref.at[source],
            dst_ref=out_ref.at[source],
            send_sem=send_sem.at[source],
            recv_sem=recv_sem.at[source],
            device_id=place(source, experts_axis),
            device_id_type=MESH,
        )

    def start(step, carry):
        copy_to(step).start()
        return carry

    def finish(step, carry):
        copy = copy_from(step)
        copy.wait_send()
        copy.wait_recv()
        return carry

    lax.fori_loop(1, n, start, 0)
    own.wait()
    lax.fori_loop(1, n, finish, 0)


def exchange(send, n, experts_axis):
    return pl.pallas_call(
        functools.partial(exchange_kernel, n, experts_axis),
        out_shape=jax.ShapeDtypeStruct(send.shape, send.dtype),
        in_specs=[pl.BlockSpec(memory_space=pltpu.VMEM)],
        out_specs=pl.BlockSpec(memory_space=pltpu.VMEM),
        scratch_shapes=[
            pltpu.SemaphoreType.DMA((n,)),
            pltpu.SemaphoreType.DMA((n,)),
            pltpu.SemaphoreType.DMA,
        ],
        compiler_params=pltpu.CompilerParams(
            collective_id=0, has_side_effects=True, vmem_limit_bytes=40 * 1024 * 1024
        ),
    )(send)


def axis_orders(n, experts_axis):
    bits = n.bit_length() - 1
    core = experts_axis.bit_length() - 1
    others = [b for b in range(bits) if b != core]
    low = others[0]
    high = others[-1]
    middle = others[1:-1]
    return core, [
        [high, low] + middle,
        [low] + middle + [high],
        middle + [high, low],
    ]


def column_groups(width):
    tiles = width // LANES
    cuts = [(tiles * g) // 3 * LANES for g in range(4)]
    return [(cuts[g], cuts[g + 1] - cuts[g]) for g in range(3)]


def gather_kernel(n, experts_axis, width, mine_ref, out_ref, *scratch):
    bits = n.bit_length() - 1
    me = flat_index(experts_axis)
    core, orders = axis_orders(n, experts_axis)
    held, send_sem, recv_sem = scratch[:3], scratch[3], scratch[4]
    for group, (first, wide) in enumerate(column_groups(width)):
        held[group][0] = mine_ref[:, first : first + wide]
    greet_bits(bits, experts_axis)
    plans = [order[::-1] + [core] for order in orders]
    for stage in range(bits):
        count = 1 << stage
        copies = []
        for group in range(3):
            bit = plans[group][stage]
            copy = pltpu.make_async_remote_copy(
                src_ref=held[group].at[pl.ds(0, count)],
                dst_ref=held[group].at[pl.ds(count, count)],
                send_sem=send_sem.at[stage, group],
                recv_sem=recv_sem.at[stage, group],
                device_id=place(flipped(me, bit), experts_axis),
                device_id_type=MESH,
            )
            copy.start()
            copies.append(copy)
        for copy in copies:
            copy.wait()
    for group, (first, wide) in enumerate(column_groups(width)):
        for slot in range(n):
            offset = sum(
                1 << plans[group][stage] for stage in range(bits) if (slot >> stage) & 1
            )
            out_ref[offset, :, first : first + wide] = held[group][slot]


def gather(mine, n, experts_axis):
    rows, width = mine.shape
    bits = n.bit_length() - 1
    return pl.pallas_call(
        functools.partial(gather_kernel, n, experts_axis, width),
        out_shape=jax.ShapeDtypeStruct((n, rows, width), mine.dtype),
        in_specs=[pl.BlockSpec(memory_space=pltpu.VMEM)],
        out_specs=pl.BlockSpec(memory_space=pltpu.VMEM),
        scratch_shapes=[
            pltpu.VMEM((n, rows, wide), mine.dtype) for _, wide in column_groups(width)
        ]
        + [pltpu.SemaphoreType.DMA((bits, 3)), pltpu.SemaphoreType.DMA((bits, 3))],
        compiler_params=pltpu.CompilerParams(
            collective_id=1, has_side_effects=True, vmem_limit_bytes=48 * 1024 * 1024
        ),
    )(mine)


def stage_types(bits):
    return [jnp.bfloat16 if stage < 3 else jnp.float32 for stage in range(bits)]


def reduce_kernel(n, experts_axis, block, width, left_ref, right_ref, out_ref, *scratch):
    bits = n.bit_length() - 1
    me = flat_index(experts_axis)
    core, orders = axis_orders(n, experts_axis)
    plans = [[core] + order for order in orders]
    groups = column_groups(width)
    types = stage_types(bits)
    kept = [[scratch[3 * (s * 3 + g)] for g in range(3)] for s in range(bits)]
    sent = [[scratch[3 * (s * 3 + g) + 1] for g in range(3)] for s in range(bits)]
    came = [[scratch[3 * (s * 3 + g) + 2] for g in range(3)] for s in range(bits)]
    send_sem, recv_sem = scratch[9 * bits], scratch[9 * bits + 1]
    greet_bits(bits, experts_axis)

    def transfer(stage, group):
        return pltpu.make_async_remote_copy(
            src_ref=sent[stage][group],
            dst_ref=came[stage][group],
            send_sem=send_sem.at[stage, group],
            recv_sem=recv_sem.at[stage, group],
            device_id=place(flipped(me, plans[group][stage]), experts_axis),
            device_id_type=MESH,
        )

    def side_of(bit):
        return (me // (1 << bit)) % 2

    chunk = experts_axis * block
    spans = n // (2 * experts_axis)

    def first_half(group, side, into, kind):
        first, wide = groups[group]
        for span in range(spans):
            at = pl.multiple_of((2 * span + side) * chunk, chunk)
            product = jnp.dot(
                left_ref[pl.ds(at, chunk), :],
                right_ref[:, first : first + wide],
                preferred_element_type=jnp.float32,
            )
            for item in range(experts_axis):
                into[span * experts_axis + item] = product[
                    item * block : (item + 1) * block
                ].astype(kind)

    for group in range(3):
        first_half(group, 1 - side_of(core), sent[0][group], types[0])
        transfer(0, group).start()
    for group in range(3):
        first_half(group, side_of(core), kept[0][group], jnp.float32)

    left = [[b for b in range(bits - 1, -1, -1) if b != core] for _ in groups]
    for stage in range(1, bits):
        half = n >> (stage + 1)
        for group in range(3):
            bit = plans[group][stage]
            low = 1 << (len(left[group]) - left[group].index(bit) - 1)
            left[group].remove(bit)
            mine = side_of(bit)

            def move(side, into, kind, low=low, stage=stage, group=group, half=half):
                def one(item, carry):
                    at = (item // low) * (2 * low) + side * low + item % low
                    into[item] = (
                        kept[stage - 1][group][at]
                        + came[stage - 1][group][at].astype(jnp.float32)
                    ).astype(kind)
                    return carry

                lax.fori_loop(0, half, one, 0)

            transfer(stage - 1, group).wait()
            move(1 - mine, sent[stage][group], types[stage])
            transfer(stage, group).start()
            move(mine, kept[stage][group], jnp.float32)
    for group, (first, wide) in enumerate(groups):
        transfer(bits - 1, group).wait()
        out_ref[:, first : first + wide] = kept[bits - 1][group][0] + came[bits - 1][group][
            0
        ].astype(jnp.float32)


def reduce_scatter(left, right, block, n, experts_axis):
    width = right.shape[1]
    bits = n.bit_length() - 1
    types = stage_types(bits)
    scratch = []
    for stage in range(bits):
        half = n >> (stage + 1)
        for _, wide in column_groups(width):
            scratch.append(pltpu.VMEM((half, block, wide), jnp.float32))
            scratch.append(pltpu.VMEM((half, block, wide), types[stage]))
            scratch.append(pltpu.VMEM((half, block, wide), types[stage]))
    return pl.pallas_call(
        functools.partial(reduce_kernel, n, experts_axis, block, width),
        out_shape=jax.ShapeDtypeStruct((block, width), jnp.float32),
        in_specs=[pl.BlockSpec(memory_space=pltpu.VMEM)] * 2,
        out_specs=pl.BlockSpec(memory_space=pltpu.VMEM),
        scratch_shapes=scratch
        + [pltpu.SemaphoreType.DMA((bits, 3)), pltpu.SemaphoreType.DMA((bits, 3))],
        compiler_params=pltpu.CompilerParams(
            collective_id=2, has_side_effects=True, vmem_limit_bytes=52 * 1024 * 1024
        ),
    )(left, right)


def lines_of(blocks, count, rows, first):
    lines = blocks.shape[0]
    wanted = jnp.arange(lines // rows * count, dtype=jnp.int32)
    wanted = wanted // count * rows + first + wanted % count
    chosen = wanted[:, None] == jnp.arange(lines, dtype=jnp.int32)[None, :]
    return jnp.dot(
        chosen.astype(jnp.bfloat16), blocks, preferred_element_type=jnp.float32
    ).astype(jnp.bfloat16)


def trunk(rows, gain, weight):
    values = rows.astype(jnp.float32)
    factor = lax.rsqrt(jnp.mean(values * values, axis=1, keepdims=True) + 1e-06)
    normed = (values * factor * gain).astype(jnp.bfloat16)
    hidden = values + jnp.dot(normed, weight, preferred_element_type=jnp.float32)
    return normed, hidden.astype(jnp.bfloat16)


def dot_t(a, b):
    return lax.dot_general(a, b, (((1,), (1,)), ((), ())), preferred_element_type=jnp.float32)


def t_dot(a, b):
    return lax.dot_general(a, b, (((0,), (0,)), ((), ())), preferred_element_type=jnp.float32)


def through_expert(hidden, cotan, gate_w, up_w, down_w):
    gate_pre = jnp.dot(hidden, gate_w, preferred_element_type=jnp.float32)
    up_pre = jnp.dot(hidden, up_w, preferred_element_type=jnp.float32)
    sigma = jax.nn.sigmoid(gate_pre)
    silu_val = gate_pre * sigma
    active = (silu_val * up_pre).astype(jnp.bfloat16)
    d_active = dot_t(cotan, down_w)
    d_gate = (d_active * up_pre * sigma * (1.0 + gate_pre * (1.0 - sigma))).astype(jnp.bfloat16)
    d_up = (d_active * silu_val).astype(jnp.bfloat16)
    d_rows = (dot_t(d_gate, gate_w) + dot_t(d_up, up_w)).astype(jnp.bfloat16)
    return active, d_gate, d_up, d_rows


def body(embeds, trunk_gain, trunk_weight, w_gate, w_up, w_down, tags, plan, helper, cotangent):
    n = lax.axis_size(("dp", "expert"))
    experts_axis = lax.axis_size("expert")
    device = flat_index(experts_axis)
    hot_expert = plan[0]
    tokens, feature = embeds.shape
    capacity = tokens // n
    hot_slots = tokens // 32
    rows = padded(2 * capacity, TILE)
    gate_w, up_w, down_w = w_gate[0], w_up[0], w_down[0]

    token = jnp.arange(tokens, dtype=jnp.int32)
    before = (helper[:, None] == helper[None, :]) & (token[:, None] > token[None, :])
    slot = jnp.sum(before.astype(jnp.int32), axis=1)
    target = helper * rows + slot
    line = jnp.arange(n * rows, dtype=jnp.int32)
    pick = jnp.concatenate(
        [line[:, None] == target[None, :], line[:, None] == target[None, :] + capacity], axis=1
    ).astype(jnp.bfloat16)
    flagged = ((tags == hot_expert) & (helper != hot_expert)).astype(jnp.bfloat16)
    flag_lanes = jnp.broadcast_to(flagged[:, None], (tokens, LANES))
    content = jnp.concatenate(
        [
            jnp.concatenate([embeds, flag_lanes], axis=1),
            jnp.concatenate([cotangent, jnp.zeros_like(flag_lanes)], axis=1),
        ],
        axis=0,
    )
    send = jnp.dot(pick, content, preferred_element_type=jnp.float32).astype(jnp.bfloat16)
    got = exchange(send.reshape(n, rows, feature + LANES), n, experts_axis)
    got = got.reshape(n * rows, feature + LANES)
    got_wide = lines_of(got, capacity, rows, 0)
    got_embeds = got_wide[:, :feature]
    got_cotan = lines_of(got[:, :feature], capacity, rows, capacity)
    flags = got_wide[:, feature] > 0

    rank = jnp.sum((flags[None, :] & (token[:, None] > token[None, :])).astype(jnp.int32), axis=1)
    picker = (rank[None, :] == jnp.arange(hot_slots, dtype=jnp.int32)[:, None]) & flags[None, :]
    picker = picker.astype(jnp.bfloat16)
    hot = jnp.concatenate(
        [
            jnp.dot(picker, got_embeds, preferred_element_type=jnp.float32),
            jnp.dot(picker, got_cotan, preferred_element_type=jnp.float32),
        ],
        axis=0,
    ).astype(jnp.bfloat16)
    pooled = gather(hot, n, experts_axis)
    pooled = pooled.reshape(n * 2 * hot_slots, feature)
    hot_embeds = lines_of(pooled, hot_slots, 2 * hot_slots, 0)
    hot_cotan = lines_of(pooled, hot_slots, 2 * hot_slots, hot_slots)
    is_owner = device == hot_expert
    hot_cotan = jnp.where(is_owner, hot_cotan, jnp.zeros_like(hot_cotan))
    own_cotan = jnp.where(flags[:, None], jnp.zeros_like(got_cotan), got_cotan)

    all_embeds = jnp.concatenate([got_embeds, hot_embeds], axis=0)
    all_cotan = jnp.concatenate([own_cotan, hot_cotan], axis=0)
    normed, hidden = trunk(all_embeds, trunk_gain, trunk_weight)
    active, d_gate, d_up, d_rows = through_expert(hidden, all_cotan, gate_w, up_w, down_w)

    share = feature // n
    block = padded(share, TILE // 2)
    column = jnp.arange(n * block, dtype=jnp.int32)
    source = jnp.where(column % block < share, column // block * share + column % block, -1)
    spread = (source[:, None] == jnp.arange(feature, dtype=jnp.int32)[None, :]).astype(
        jnp.bfloat16
    )
    normed_lines = dot_t(spread, normed).astype(jnp.bfloat16)
    grad_trunk = reduce_scatter(normed_lines, d_rows, block, n, experts_axis)[:share]

    grad_gate = t_dot(hidden, d_gate).astype(jnp.bfloat16)[None]
    grad_up = t_dot(hidden, d_up).astype(jnp.bfloat16)[None]
    grad_down = t_dot(active, all_cotan).astype(jnp.bfloat16)[None]
    return (grad_gate, grad_up, grad_down, grad_trunk)


def bit_of(me, bit):
    return (me // (1 << bit)) % 2


def iota(shape, dim):
    return lax.broadcasted_iota(jnp.int32, shape, dim)


def as_ones(mask, kind=jnp.bfloat16):
    return jnp.where(mask, 1.0, 0.0).astype(kind)


def reduce_orders(n, experts_axis):
    bits = n.bit_length() - 1
    core = experts_axis.bit_length() - 1
    others = [b for b in range(bits) if b != core]
    low, high, middle = others[0], others[-1], others[1:-1]
    return [core, high, low] + middle, [core, low, high] + middle


def reduce_widths(width):
    widths = [2 * LANES] * (width // (2 * LANES))
    if width % (2 * LANES):
        widths.append(width % (2 * LANES))
    starts = [sum(widths[:g]) for g in range(len(widths))]
    return list(zip(starts, widths))


def fused_kernel(n, experts_axis, hot_slots, names, *refs):
    plain, tree = names
    r = types.SimpleNamespace(
        **dict(zip(plain, refs)), **jax.tree.unflatten(tree, refs[len(plain) :])
    )
    bits = n.bit_length() - 1
    tokens, feature = r.emb.shape
    hidden_units = r.wg.shape[1]
    capacity = tokens // n
    hot_rows = n * hot_slots
    share = feature // n
    me = flat_index(experts_axis)
    wide_groups = column_groups(feature)
    core, gather_orders = axis_orders(n, experts_axis)
    gather_plans = [order[::-1] + [core] for order in gather_orders]
    reduce_groups = reduce_widths(feature)
    orders = reduce_orders(n, experts_axis)
    layout = orders[0]

    barrier = pltpu.get_barrier_semaphore()

    def greet(step, carry):
        pl.semaphore_signal(
            barrier,
            inc=1,
            device_id=place(lax.rem(me + step, n), experts_axis),
            device_id_type=MESH,
        )
        return carry

    pairs = (
        (r.tags_hbm, r.tags),
        (r.plan_hbm, r.plan),
        (r.helper_hbm, r.helper),
        (r.emb_hbm, r.emb),
        (r.cot_hbm, r.cot),
        (r.gain_hbm, r.gain),
        (r.tw_hbm, r.tw),
        (r.wg_hbm.at[0], r.wg),
        (r.wu_hbm.at[0], r.wu),
        (r.wd_hbm.at[0], r.wd),
    )
    loads = [
        pltpu.make_async_copy(far, near, r.load_sem.at[index])
        for index, (far, near) in enumerate(pairs)
    ]
    for load in loads[:4]:
        load.start()
    lax.fori_loop(1, n, greet, 0)
    for load in loads[4:]:
        load.start()
    for load in loads[:3]:
        load.wait()

    helper = r.helper[...]
    popular = r.plan[0:1, 0:1]
    foreign = (r.tags[...] == popular) & (helper != popular)
    to_device = iota((n, tokens), 0) == helper
    ahead = as_ones(iota((tokens, tokens), 0) < iota((tokens, tokens), 1))
    to_ones = as_ones(to_device)
    count = jnp.dot(to_ones, ahead, preferred_element_type=jnp.float32)
    slot = jnp.sum(jnp.where(to_device, count, 0.0), axis=0, keepdims=True).astype(jnp.int32)
    target = helper * capacity + slot
    pick = as_ones(iota((tokens, tokens), 0) == target)
    marked = as_ones((iota((LANES, tokens), 0) == slot) & foreign)
    marks = dot_t(to_ones, marked)
    for device in range(n):
        r.out[MARK][device] = marks[device : device + 1]

    def packed(whole):
        rows = jnp.dot(pick, whole[...], preferred_element_type=jnp.float32)
        return rows.reshape(n, capacity, feature).astype(jnp.bfloat16)

    loads[3].wait()
    r.out[EMB][...] = packed(r.emb)

    def exchange_copy(kind, step, arriving):
        other = lax.rem(me + step, n)
        return pltpu.make_async_remote_copy(
            src_ref=r.out[kind].at[other],
            dst_ref=r.into[kind].at[other if arriving else me],
            send_sem=r.send_sem.at[kind, other],
            recv_sem=r.recv_sem.at[kind, other if arriving else me],
            device_id=place(other, experts_axis),
            device_id_type=MESH,
        )

    def start_kinds(first, last, *some):
        def start(step, carry):
            for kind in some:
                exchange_copy(kind, step, False).start()
            return carry

        lax.fori_loop(first, last, start, 0)

    def start_batch(batch):
        cuts = [1 + (n - 1) * at // (bits + 1) for at in range(bits + 2)]
        start_kinds(cuts[batch], cuts[batch + 1], COT)

    def finish_kind(kind):
        def finish(step, carry):
            copy = exchange_copy(kind, step, True)
            copy.wait_send()
            copy.wait_recv()
            return carry

        lax.fori_loop(1, n, finish, 0)

    own = [
        pltpu.make_async_copy(r.out[kind].at[me], r.into[kind].at[me], r.own_sem.at[kind])
        for kind in (MARK, EMB, COT)
    ]

    pl.semaphore_wait(barrier, n - 1)
    start_kinds(1, n, MARK, EMB)
    own[MARK].start()
    own[EMB].start()
    loads[4].wait()
    r.out[COT][...] = packed(r.cot)
    start_batch(0)
    own[COT].start()

    place_row = iota((feature, 1), 0)
    block = jnp.floor((place_row.astype(jnp.float32) + 0.5) / share).astype(jnp.int32)
    source = place_row - block * share
    for position, bit in enumerate(layout):
        part = jnp.right_shift(block, bits - 1 - position) & 1
        source = source + part * (share << bit)
    r.order[...] = as_ones(source == iota((feature, feature), 1))

    def gather_copy(kind, stage, group):
        held = r.held[kind - EMB][group]
        size = 1 << stage
        return pltpu.make_async_remote_copy(
            src_ref=held.at[pl.ds(0, size)],
            dst_ref=held.at[pl.ds(size, size)],
            send_sem=r.gather_send.at[kind - EMB, stage, group],
            recv_sem=r.gather_recv.at[kind - EMB, stage, group],
            device_id=place(flipped(me, gather_plans[group][stage]), experts_axis),
            device_id_type=MESH,
        )

    def gather_begin(kind, rows):
        for group, (first, wide) in enumerate(wide_groups):
            r.held[kind - EMB][group][0] = rows[:, first : first + wide].astype(jnp.bfloat16)
        for group in range(3):
            gather_copy(kind, 0, group).start()

    def gather_step(kind, stage):
        for group in range(3):
            gather_copy(kind, stage, group).wait()
        if stage + 1 < bits:
            for group in range(3):
                gather_copy(kind, stage + 1, group).start()

    def gathered(kind, group):
        plan = gather_plans[group]
        held = r.held[kind - EMB][group]
        parts = []
        for offset in range(n):
            at = sum(1 << stage for stage in range(bits) if (offset >> plan[stage]) & 1)
            parts.append(held[at].astype(jnp.float32))
        return jnp.concatenate(parts, axis=0)

    def unpacked(kind):
        return r.into[kind][...].astype(jnp.float32).reshape(tokens, feature)

    def trunk_rows(values, first, rows):
        factor = lax.rsqrt(jnp.mean(values * values, axis=1, keepdims=True) + 1e-06)
        normed = (values * factor * r.gain[...].reshape(1, feature)).astype(jnp.bfloat16)
        hidden = values + jnp.dot(normed, r.tw[...], preferred_element_type=jnp.float32)
        r.hidden[first : first + rows, :] = hidden.astype(jnp.bfloat16)
        r.normed[:, first : first + rows] = dot_t(r.order[...], normed).astype(
            jnp.bfloat16
        )

    def forward_rows(first, rows):
        hidden = r.hidden[first : first + rows, :]
        r.gate[first : first + rows, :] = jnp.dot(
            hidden, r.wg[...], preferred_element_type=jnp.float32
        )
        r.up[first : first + rows, :] = jnp.dot(
            hidden, r.wu[...], preferred_element_type=jnp.float32
        )

    def backward_rows(first, rows):
        d_active = dot_t(r.cotan[first : first + rows, :], r.wd[...])
        gate_pre = r.gate[first : first + rows, :]
        up_pre = r.up[first : first + rows, :]
        sigma = jax.nn.sigmoid(gate_pre)
        silu_val = gate_pre * sigma
        r.active[first : first + rows, :] = (silu_val * up_pre).astype(jnp.bfloat16)
        r.d_gate[first : first + rows, :] = (
            d_active * up_pre * sigma * (1.0 + gate_pre * (1.0 - sigma))
        ).astype(jnp.bfloat16)
        r.d_up[first : first + rows, :] = (d_active * silu_val).astype(jnp.bfloat16)

    def rows_back(first, rows, column, wide):
        r.d_rows[first : first + rows, column : column + wide] = (
            dot_t(r.d_gate[first : first + rows, :], r.wg[column : column + wide, :])
            + dot_t(r.d_up[first : first + rows, :], r.wu[column : column + wide, :])
        ).astype(jnp.bfloat16)

    for load in loads[5:]:
        load.wait()
    own[MARK].wait()
    own[EMB].wait()
    finish_kind(MARK)
    finish_kind(EMB)

    by_source = as_ones(
        jnp.floor((iota((tokens, n), 0).astype(jnp.float32) + 0.5) / capacity).astype(jnp.int32)
        == iota((tokens, n), 1)
    )
    marks_in = jnp.concatenate([r.into[MARK][device] for device in range(n)], axis=0)
    spread = jnp.dot(by_source, marks_in.astype(jnp.bfloat16), preferred_element_type=jnp.float32)
    lane = iota((tokens, LANES), 1)
    within = iota((tokens, LANES), 0) & (capacity - 1)
    flag = jnp.sum(jnp.where(lane == within, spread, 0.0), axis=1, keepdims=True)
    before = as_ones(iota((tokens, tokens), 1) < iota((tokens, tokens), 0))
    flag_wide = jnp.broadcast_to(flag, (tokens, LANES))
    rank = jnp.dot(before, flag_wide.astype(jnp.bfloat16), preferred_element_type=jnp.float32)
    chosen = jnp.where(rank.astype(jnp.int32) == lane, flag_wide, 0.0)
    chooser = chosen.T[:hot_slots].astype(jnp.bfloat16)

    got = unpacked(EMB)
    gather_begin(EMB, jnp.dot(chooser, got.astype(jnp.bfloat16), preferred_element_type=jnp.float32))
    start_batch(1)
    trunk_rows(got, 0, tokens)
    for stage in range(bits):
        gather_step(EMB, stage)
        if stage + 1 < bits:
            start_batch(stage + 2)
        if stage == 0:
            forward_rows(0, tokens)

    hot = jnp.concatenate([gathered(EMB, group) for group in range(3)], axis=1)
    trunk_rows(hot, tokens, hot_rows)
    forward_rows(tokens, hot_rows)

    own[COT].wait()
    finish_kind(COT)
    got = unpacked(COT)
    gather_begin(COT, jnp.dot(chooser, got.astype(jnp.bfloat16), preferred_element_type=jnp.float32))
    r.cotan[0:tokens, :] = jnp.where(flag > 0, 0.0, got).astype(jnp.bfloat16)
    backward_rows(0, tokens)
    gather_step(COT, 0)
    rows_back(0, tokens, 0, feature)
    for stage in range(1, bits):
        gather_step(COT, stage)
    is_owner = popular == me
    for group, (column, wide) in enumerate(wide_groups):
        r.cotan[tokens : tokens + hot_rows, column : column + wide] = jnp.where(
            is_owner, gathered(COT, group), 0.0
        ).astype(jnp.bfloat16)
    backward_rows(tokens, hot_rows)

    def reduce_copy(stage, group):
        bit = orders[group % 2][stage]
        return pltpu.make_async_remote_copy(
            src_ref=r.sent[stage][group],
            dst_ref=r.came[stage][group],
            send_sem=r.reduce_send.at[stage, group],
            recv_sem=r.reduce_recv.at[stage, group],
            device_id=place(flipped(me, bit), experts_axis),
            device_id_type=MESH,
        )

    def pieces(stage, group, side):
        size = feature >> (stage + 1)
        bit = orders[group % 2][stage]
        if stage == 1 and bit != layout[1]:
            step = size // 2
            return [(pl.multiple_of(part * size + side * step, 16), part * step, step) for part in range(2)]
        return [(pl.multiple_of(side * size, size & -size), 0, size)]

    def reduce_step(stage, group):
        side = bit_of(me, orders[group % 2][stage])
        kept, came = r.kept[stage - 1][group], r.came[stage - 1][group]
        size = feature >> (stage + 1)
        reduce_copy(stage - 1, group).wait()
        if size % TILE:
            total = kept[0 : 2 * size] + came[0 : 2 * size].astype(jnp.float32)
            first, second = total[:size], total[size:]
            r.sent[stage][group][0:size] = jnp.where(side == 1, first, second).astype(
                jnp.bfloat16
            )
            reduce_copy(stage, group).start()
            r.kept[stage][group][0:size] = jnp.where(side == 1, second, first)
            return
        for at, into, rows in pieces(stage, group, 1 - side):
            r.sent[stage][group][into : into + rows] = (
                kept[pl.ds(at, rows)] + came[pl.ds(at, rows)].astype(jnp.float32)
            ).astype(jnp.bfloat16)
        reduce_copy(stage, group).start()
        for at, into, rows in pieces(stage, group, side):
            r.kept[stage][group][into : into + rows] = kept[pl.ds(at, rows)] + came[
                pl.ds(at, rows)
            ].astype(jnp.float32)

    side = bit_of(me, core)
    half = feature // 2

    def product(group, which):
        column, wide = reduce_groups[group]
        return jnp.dot(
            r.normed[pl.ds(pl.multiple_of(which * half, half & -half), half), :],
            r.d_rows[:, column : column + wide],
            preferred_element_type=jnp.float32,
        )

    groups = range(len(reduce_groups))
    rows_back(tokens, hot_rows, 0, feature)
    for group in groups:
        r.sent[0][group][...] = product(group, 1 - side).astype(jnp.bfloat16)
        reduce_copy(0, group).start()
        r.kept[0][group][...] = product(group, side)

    work = []
    for into, left, right in (
        (r.grad_gate, r.hidden, r.d_gate),
        (r.grad_up, r.hidden, r.d_up),
        (r.grad_down, r.active, r.cotan),
    ):
        lines = into.shape[1]
        for at, wide in reduce_widths(lines):

            def one(into=into, left=left, right=right, at=at, wide=wide):
                into[0, at : at + wide, :] = t_dot(
                    left[:, at : at + wide], right[...]
                ).astype(jnp.bfloat16)

            work.append(one)
    slots = (bits - 1) * len(reduce_groups)
    done = 0
    for stage in range(1, bits):
        for group in groups:
            reduce_step(stage, group)
            slot_index = (stage - 1) * len(reduce_groups) + group + 1
            while done < len(work) * slot_index // slots:
                work[done]()
                done += 1
    for group in groups:
        column, wide = reduce_groups[group]
        reduce_copy(bits - 1, group).wait()
        r.grad_trunk[:, column : column + wide] = r.kept[bits - 1][group][
            0:share
        ] + r.came[bits - 1][group][0:share].astype(jnp.float32)


def fused_plan(n, hot_slots, tokens, feature, units):
    bits = n.bit_length() - 1
    rows = tokens + n * hot_slots
    capacity = tokens // n
    groups = reduce_widths(feature)
    bf, f32 = jnp.bfloat16, jnp.float32
    message = pltpu.VMEM((n, capacity, feature), bf)
    mark = pltpu.VMEM((n, 1, LANES), f32)

    def stages(kind):
        sizes = [feature >> (stage + 1) for stage in range(bits)]
        return [
            [pltpu.VMEM((padded(size, TILE // 2), wide), kind) for _, wide in groups]
            for size in sizes
        ]

    return dict(
        tags=pltpu.VMEM((1, tokens), jnp.int32),
        plan=pltpu.VMEM((1, n), jnp.int32),
        helper=pltpu.VMEM((1, tokens), jnp.int32),
        gain=pltpu.VMEM((feature,), f32),
        emb=pltpu.VMEM((tokens, feature), bf),
        cot=pltpu.VMEM((tokens, feature), bf),
        tw=pltpu.VMEM((feature, feature), bf),
        wg=pltpu.VMEM((feature, units), bf),
        wu=pltpu.VMEM((feature, units), bf),
        wd=pltpu.VMEM((units, feature), bf),
        out=[mark, message, message],
        into=[mark, message, message],
        order=pltpu.VMEM((feature, feature), bf),
        hidden=pltpu.VMEM((rows, feature), bf),
        normed=pltpu.VMEM((feature, rows), bf),
        cotan=pltpu.VMEM((rows, feature), bf),
        gate=pltpu.VMEM((rows, units), f32),
        up=pltpu.VMEM((rows, units), f32),
        active=pltpu.VMEM((rows, units), bf),
        d_gate=pltpu.VMEM((rows, units), bf),
        d_up=pltpu.VMEM((rows, units), bf),
        d_rows=pltpu.VMEM((rows, feature), bf),
        held=[
            [pltpu.VMEM((n, hot_slots, wide), bf) for _, wide in column_groups(feature)]
            for _ in (EMB, COT)
        ],
        kept=stages(f32),
        sent=stages(bf),
        came=stages(bf),
        load_sem=pltpu.SemaphoreType.DMA((10,)),
        own_sem=pltpu.SemaphoreType.DMA((3,)),
        send_sem=pltpu.SemaphoreType.DMA((3, n)),
        recv_sem=pltpu.SemaphoreType.DMA((3, n)),
        gather_send=pltpu.SemaphoreType.DMA((2, bits, 3)),
        gather_recv=pltpu.SemaphoreType.DMA((2, bits, 3)),
        reduce_send=pltpu.SemaphoreType.DMA((bits, len(groups))),
        reduce_recv=pltpu.SemaphoreType.DMA((bits, len(groups))),
    )


def plan_bytes(plan):
    total = 0
    for item in jax.tree.leaves(plan):
        if len(item.shape) > 1 and item.shape[-1] % LANES == 0:
            lead = 1
            for size in item.shape[:-2]:
                lead *= size
            lines = padded(item.shape[-2], TILE // 2)
            total += lead * lines * item.shape[-1] * jnp.dtype(item.dtype).itemsize
    return total


def settle_kernel(count, *refs):
    sems = refs[-1]
    copies = [
        pltpu.make_async_copy(refs[at], refs[count + at], sems.at[at]) for at in range(count)
    ]
    for copy in copies:
        copy.start()
    for copy in copies:
        copy.wait()


def settle(arrays):
    return pl.pallas_call(
        functools.partial(settle_kernel, len(arrays)),
        out_shape=tuple(jax.ShapeDtypeStruct(array.shape, array.dtype) for array in arrays),
        in_specs=[pl.BlockSpec(memory_space=pl.ANY)] * len(arrays),
        out_specs=(pl.BlockSpec(memory_space=pltpu.HBM),) * len(arrays),
        scratch_shapes=[pltpu.SemaphoreType.DMA((len(arrays),))],
        compiler_params=pltpu.CompilerParams(vmem_limit_bytes=1024 * 1024),
    )(*arrays)


def fused_body(embeds, trunk_gain, trunk_weight, w_gate, w_up, w_down, tags, plan, helper, cotangent):
    n = lax.axis_size(("dp", "expert"))
    experts_axis = lax.axis_size("expert")
    tokens, feature = embeds.shape
    units = w_gate.shape[2]
    hot_slots = tokens // 32
    anywhere = pl.BlockSpec(memory_space=pltpu.HBM)
    inside = pl.BlockSpec(memory_space=pltpu.VMEM)
    inputs = dict(
        emb_hbm=(embeds, anywhere),
        gain_hbm=(trunk_gain, anywhere),
        tw_hbm=(trunk_weight, anywhere),
        wg_hbm=(w_gate, anywhere),
        wu_hbm=(w_up, anywhere),
        wd_hbm=(w_down, anywhere),
        tags_hbm=(tags.reshape(1, tokens), anywhere),
        plan_hbm=(plan.reshape(1, -1), anywhere),
        helper_hbm=(helper.reshape(1, tokens), anywhere),
        cot_hbm=(cotangent, anywhere),
    )
    outputs = dict(
        grad_gate=jax.ShapeDtypeStruct(w_gate.shape, jnp.bfloat16),
        grad_up=jax.ShapeDtypeStruct(w_up.shape, jnp.bfloat16),
        grad_down=jax.ShapeDtypeStruct(w_down.shape, jnp.bfloat16),
        grad_trunk=jax.ShapeDtypeStruct((feature // n, feature), jnp.float32),
    )
    scratch = fused_plan(n, hot_slots, tokens, feature, units)
    names = (list(inputs) + list(outputs), jax.tree.structure(scratch))
    results = pl.pallas_call(
        functools.partial(fused_kernel, n, experts_axis, hot_slots, names),
        out_shape=tuple(outputs.values()),
        in_specs=[spec for _, spec in inputs.values()],
        out_specs=(inside,) * len(outputs),
        scratch_shapes=jax.tree.leaves(scratch),
        compiler_params=pltpu.CompilerParams(
            collective_id=0, has_side_effects=True, vmem_limit_bytes=VMEM_BYTES
        ),
    )(*[pltpu.with_memory_space_constraint(value, pltpu.HBM) for value, _ in inputs.values()])
    return settle(results)


def fits(embeds, w_gate, n):
    tokens, feature = embeds.shape
    units = w_gate.shape[2]
    hot_slots = tokens // 32
    if (tokens // n) % 8 or hot_slots % 8 or feature % (16 * n // 4):
        return False
    return plan_bytes(fused_plan(n, hot_slots, tokens, feature, units)) < VMEM_BYTES - 2 * 1024 * 1024


def either(*args):
    n = lax.axis_size(("dp", "expert"))
    return (fused_body if fits(args[0], args[3], n) else body)(*args)


def solution(mesh):
    spread_rows = P(("dp", "expert"), None)
    spread_first = P(("dp", "expert"), None, None)
    return jax.shard_map(
        either,
        mesh=mesh,
        in_specs=(
            spread_rows,
            P(),
            P(),
            spread_first,
            spread_first,
            spread_first,
            P(("dp", "expert")),
            P(),
            P(("dp", "expert")),
            spread_rows,
        ),
        out_specs=(spread_first, spread_first, spread_first, spread_rows),
        check_vma=False,
    )
```

```python
import functools
import types

import jax
import jax.numpy as jnp
from jax import lax
from jax.experimental import pallas as pl
from jax.experimental.pallas import tpu as pltpu
from jax.sharding import PartitionSpec as P

LANES = 128
TILE = 16
MESH = pl.DeviceIdType.MESH
MARK, EMB, COT = range(3)
WAVE = 99
VMEM_BYTES = 45 * 1024 * 1024


def padded(value, multiple):
    return -(-value // multiple) * multiple


def flat_index(experts_axis):
    return lax.axis_index("dp") * experts_axis + lax.axis_index("expert")


def place(flat, experts_axis):
    return (flat // experts_axis, flat % experts_axis)


def flipped(me, bit):
    weight = 1 << bit
    return me + (1 - 2 * ((me // weight) % 2)) * weight


def greet_all(n, experts_axis):
    me = flat_index(experts_axis)
    barrier = pltpu.get_barrier_semaphore()

    def greet(step, carry):
        pl.semaphore_signal(
            barrier,
            inc=1,
            device_id=place(lax.rem(me + step, n), experts_axis),
            device_id_type=MESH,
        )
        return carry

    lax.fori_loop(1, n, greet, 0)
    pl.semaphore_wait(barrier, n - 1)


def greet_bits(bits, experts_axis):
    me = flat_index(experts_axis)
    barrier = pltpu.get_barrier_semaphore()
    for bit in range(bits):
        pl.semaphore_signal(
            barrier, inc=1, device_id=place(flipped(me, bit), experts_axis), device_id_type=MESH
        )
    pl.semaphore_wait(barrier, bits)


def exchange_kernel(n, experts_axis, send_ref, out_ref, send_sem, recv_sem, own_sem):
    me = flat_index(experts_axis)
    greet_all(n, experts_axis)
    own = pltpu.make_async_copy(send_ref.at[me], out_ref.at[me], own_sem)
    own.start()

    def copy_to(step):
        to = lax.rem(me + step, n)
        return pltpu.make_async_remote_copy(
            src_ref=send_ref.at[to],
            dst_ref=out_ref.at[me],
            send_sem=send_sem.at[to],
            recv_sem=recv_sem.at[me],
            device_id=place(to, experts_axis),
            device_id_type=MESH,
        )

    def copy_from(step):
        source = lax.rem(me + step, n)
        return pltpu.make_async_remote_copy(
            src_ref=send_ref.at[source],
            dst_ref=out_ref.at[source],
            send_sem=send_sem.at[source],
            recv_sem=recv_sem.at[source],
            device_id=place(source, experts_axis),
            device_id_type=MESH,
        )

    def start(step, carry):
        copy_to(step).start()
        return carry

    def finish(step, carry):
        copy = copy_from(step)
        copy.wait_send()
        copy.wait_recv()
        return carry

    lax.fori_loop(1, n, start, 0)
    own.wait()
    lax.fori_loop(1, n, finish, 0)


def exchange(send, n, experts_axis):
    return pl.pallas_call(
        functools.partial(exchange_kernel, n, experts_axis),
        out_shape=jax.ShapeDtypeStruct(send.shape, send.dtype),
        in_specs=[pl.BlockSpec(memory_space=pltpu.VMEM)],
        out_specs=pl.BlockSpec(memory_space=pltpu.VMEM),
        scratch_shapes=[
            pltpu.SemaphoreType.DMA((n,)),
            pltpu.SemaphoreType.DMA((n,)),
            pltpu.SemaphoreType.DMA,
        ],
        compiler_params=pltpu.CompilerParams(
            collective_id=0, has_side_effects=True, vmem_limit_bytes=40 * 1024 * 1024
        ),
    )(send)


def axis_orders(n, experts_axis):
    bits = n.bit_length() - 1
    core = experts_axis.bit_length() - 1
    others = [b for b in range(bits) if b != core]
    low = others[0]
    high = others[-1]
    middle = others[1:-1]
    return core, [
        [high, low] + middle,
        [low] + middle + [high],
        middle + [high, low],
    ]


def column_groups(width):
    tiles = width // LANES
    cuts = [(tiles * g) // 3 * LANES for g in range(4)]
    return [(cuts[g], cuts[g + 1] - cuts[g]) for g in range(3)]


def gather_kernel(n, experts_axis, width, mine_ref, out_ref, *scratch):
    bits = n.bit_length() - 1
    me = flat_index(experts_axis)
    core, orders = axis_orders(n, experts_axis)
    held, send_sem, recv_sem = scratch[:3], scratch[3], scratch[4]
    for group, (first, wide) in enumerate(column_groups(width)):
        held[group][0] = mine_ref[:, first : first + wide]
    greet_bits(bits, experts_axis)
    plans = [order[::-1] + [core] for order in orders]
    for stage in range(bits):
        count = 1 << stage
        copies = []
        for group in range(3):
            bit = plans[group][stage]
            copy = pltpu.make_async_remote_copy(
                src_ref=held[group].at[pl.ds(0, count)],
                dst_ref=held[group].at[pl.ds(count, count)],
                send_sem=send_sem.at[stage, group],
                recv_sem=recv_sem.at[stage, group],
                device_id=place(flipped(me, bit), experts_axis),
                device_id_type=MESH,
            )
            copy.start()
            copies.append(copy)
        for copy in copies:
            copy.wait()
    for group, (first, wide) in enumerate(column_groups(width)):
        for slot in range(n):
            offset = sum(
                1 << plans[group][stage] for stage in range(bits) if (slot >> stage) & 1
            )
            out_ref[offset, :, first : first + wide] = held[group][slot]


def gather(mine, n, experts_axis):
    rows, width = mine.shape
    bits = n.bit_length() - 1
    return pl.pallas_call(
        functools.partial(gather_kernel, n, experts_axis, width),
        out_shape=jax.ShapeDtypeStruct((n, rows, width), mine.dtype),
        in_specs=[pl.BlockSpec(memory_space=pltpu.VMEM)],
        out_specs=pl.BlockSpec(memory_space=pltpu.VMEM),
        scratch_shapes=[
            pltpu.VMEM((n, rows, wide), mine.dtype) for _, wide in column_groups(width)
        ]
        + [pltpu.SemaphoreType.DMA((bits, 3)), pltpu.SemaphoreType.DMA((bits, 3))],
        compiler_params=pltpu.CompilerParams(
            collective_id=1, has_side_effects=True, vmem_limit_bytes=48 * 1024 * 1024
        ),
    )(mine)


def stage_types(bits):
    return [jnp.bfloat16 if stage < 3 else jnp.float32 for stage in range(bits)]


def reduce_kernel(n, experts_axis, block, width, left_ref, right_ref, out_ref, *scratch):
    bits = n.bit_length() - 1
    me = flat_index(experts_axis)
    core, orders = axis_orders(n, experts_axis)
    plans = [[core] + order for order in orders]
    groups = column_groups(width)
    types = stage_types(bits)
    kept = [[scratch[3 * (s * 3 + g)] for g in range(3)] for s in range(bits)]
    sent = [[scratch[3 * (s * 3 + g) + 1] for g in range(3)] for s in range(bits)]
    came = [[scratch[3 * (s * 3 + g) + 2] for g in range(3)] for s in range(bits)]
    send_sem, recv_sem = scratch[9 * bits], scratch[9 * bits + 1]
    greet_bits(bits, experts_axis)

    def transfer(stage, group):
        return pltpu.make_async_remote_copy(
            src_ref=sent[stage][group],
            dst_ref=came[stage][group],
            send_sem=send_sem.at[stage, group],
            recv_sem=recv_sem.at[stage, group],
            device_id=place(flipped(me, plans[group][stage]), experts_axis),
            device_id_type=MESH,
        )

    def side_of(bit):
        return (me // (1 << bit)) % 2

    chunk = experts_axis * block
    spans = n // (2 * experts_axis)

    def first_half(group, side, into, kind):
        first, wide = groups[group]
        for span in range(spans):
            at = pl.multiple_of((2 * span + side) * chunk, chunk)
            product = jnp.dot(
                left_ref[pl.ds(at, chunk), :],
                right_ref[:, first : first + wide],
                preferred_element_type=jnp.float32,
            )
            for item in range(experts_axis):
                into[span * experts_axis + item] = product[
                    item * block : (item + 1) * block
                ].astype(kind)

    for group in range(3):
        first_half(group, 1 - side_of(core), sent[0][group], types[0])
        transfer(0, group).start()
    for group in range(3):
        first_half(group, side_of(core), kept[0][group], jnp.float32)

    left = [[b for b in range(bits - 1, -1, -1) if b != core] for _ in groups]
    for stage in range(1, bits):
        half = n >> (stage + 1)
        for group in range(3):
            bit = plans[group][stage]
            low = 1 << (len(left[group]) - left[group].index(bit) - 1)
            left[group].remove(bit)
            mine = side_of(bit)

            def move(side, into, kind, low=low, stage=stage, group=group, half=half):
                def one(item, carry):
                    at = (item // low) * (2 * low) + side * low + item % low
                    into[item] = (
                        kept[stage - 1][group][at]
                        + came[stage - 1][group][at].astype(jnp.float32)
                    ).astype(kind)
                    return carry

                lax.fori_loop(0, half, one, 0)

            transfer(stage - 1, group).wait()
            move(1 - mine, sent[stage][group], types[stage])
            transfer(stage, group).start()
            move(mine, kept[stage][group], jnp.float32)
    for group, (first, wide) in enumerate(groups):
        transfer(bits - 1, group).wait()
        out_ref[:, first : first + wide] = kept[bits - 1][group][0] + came[bits - 1][group][
            0
        ].astype(jnp.float32)


def reduce_scatter(left, right, block, n, experts_axis):
    width = right.shape[1]
    bits = n.bit_length() - 1
    types = stage_types(bits)
    scratch = []
    for stage in range(bits):
        half = n >> (stage + 1)
        for _, wide in column_groups(width):
            scratch.append(pltpu.VMEM((half, block, wide), jnp.float32))
            scratch.append(pltpu.VMEM((half, block, wide), types[stage]))
            scratch.append(pltpu.VMEM((half, block, wide), types[stage]))
    return pl.pallas_call(
        functools.partial(reduce_kernel, n, experts_axis, block, width),
        out_shape=jax.ShapeDtypeStruct((block, width), jnp.float32),
        in_specs=[pl.BlockSpec(memory_space=pltpu.VMEM)] * 2,
        out_specs=pl.BlockSpec(memory_space=pltpu.VMEM),
        scratch_shapes=scratch
        + [pltpu.SemaphoreType.DMA((bits, 3)), pltpu.SemaphoreType.DMA((bits, 3))],
        compiler_params=pltpu.CompilerParams(
            collective_id=2, has_side_effects=True, vmem_limit_bytes=52 * 1024 * 1024
        ),
    )(left, right)


def lines_of(blocks, count, rows, first):
    lines = blocks.shape[0]
    wanted = jnp.arange(lines // rows * count, dtype=jnp.int32)
    wanted = wanted // count * rows + first + wanted % count
    chosen = wanted[:, None] == jnp.arange(lines, dtype=jnp.int32)[None, :]
    return jnp.dot(
        chosen.astype(jnp.bfloat16), blocks, preferred_element_type=jnp.float32
    ).astype(jnp.bfloat16)


def trunk(rows, gain, weight):
    values = rows.astype(jnp.float32)
    factor = lax.rsqrt(jnp.mean(values * values, axis=1, keepdims=True) + 1e-06)
    normed = (values * factor * gain).astype(jnp.bfloat16)
    hidden = values + jnp.dot(normed, weight, preferred_element_type=jnp.float32)
    return normed, hidden.astype(jnp.bfloat16)


def dot_t(a, b):
    return lax.dot_general(a, b, (((1,), (1,)), ((), ())), preferred_element_type=jnp.float32)


def t_dot(a, b):
    return lax.dot_general(a, b, (((0,), (0,)), ((), ())), preferred_element_type=jnp.float32)


def through_expert(hidden, cotan, gate_w, up_w, down_w):
    gate_pre = jnp.dot(hidden, gate_w, preferred_element_type=jnp.float32)
    up_pre = jnp.dot(hidden, up_w, preferred_element_type=jnp.float32)
    sigma = jax.nn.sigmoid(gate_pre)
    silu_val = gate_pre * sigma
    active = (silu_val * up_pre).astype(jnp.bfloat16)
    d_active = dot_t(cotan, down_w)
    d_gate = (d_active * up_pre * sigma * (1.0 + gate_pre * (1.0 - sigma))).astype(jnp.bfloat16)
    d_up = (d_active * silu_val).astype(jnp.bfloat16)
    d_rows = (dot_t(d_gate, gate_w) + dot_t(d_up, up_w)).astype(jnp.bfloat16)
    return active, d_gate, d_up, d_rows


def body(embeds, trunk_gain, trunk_weight, w_gate, w_up, w_down, tags, plan, helper, cotangent):
    n = lax.axis_size(("dp", "expert"))
    experts_axis = lax.axis_size("expert")
    device = flat_index(experts_axis)
    hot_expert = plan[0]
    tokens, feature = embeds.shape
    capacity = tokens // n
    hot_slots = tokens // 32
    rows = padded(2 * capacity, TILE)
    gate_w, up_w, down_w = w_gate[0], w_up[0], w_down[0]

    token = jnp.arange(tokens, dtype=jnp.int32)
    before = (helper[:, None] == helper[None, :]) & (token[:, None] > token[None, :])
    slot = jnp.sum(before.astype(jnp.int32), axis=1)
    target = helper * rows + slot
    line = jnp.arange(n * rows, dtype=jnp.int32)
    pick = jnp.concatenate(
        [line[:, None] == target[None, :], line[:, None] == target[None, :] + capacity], axis=1
    ).astype(jnp.bfloat16)
    flagged = ((tags == hot_expert) & (helper != hot_expert)).astype(jnp.bfloat16)
    flag_lanes = jnp.broadcast_to(flagged[:, None], (tokens, LANES))
    content = jnp.concatenate(
        [
            jnp.concatenate([embeds, flag_lanes], axis=1),
            jnp.concatenate([cotangent, jnp.zeros_like(flag_lanes)], axis=1),
        ],
        axis=0,
    )
    send = jnp.dot(pick, content, preferred_element_type=jnp.float32).astype(jnp.bfloat16)
    got = exchange(send.reshape(n, rows, feature + LANES), n, experts_axis)
    got = got.reshape(n * rows, feature + LANES)
    got_wide = lines_of(got, capacity, rows, 0)
    got_embeds = got_wide[:, :feature]
    got_cotan = lines_of(got[:, :feature], capacity, rows, capacity)
    flags = got_wide[:, feature] > 0

    rank = jnp.sum((flags[None, :] & (token[:, None] > token[None, :])).astype(jnp.int32), axis=1)
    picker = (rank[None, :] == jnp.arange(hot_slots, dtype=jnp.int32)[:, None]) & flags[None, :]
    picker = picker.astype(jnp.bfloat16)
    hot = jnp.concatenate(
        [
            jnp.dot(picker, got_embeds, preferred_element_type=jnp.float32),
            jnp.dot(picker, got_cotan, preferred_element_type=jnp.float32),
        ],
        axis=0,
    ).astype(jnp.bfloat16)
    pooled = gather(hot, n, experts_axis)
    pooled = pooled.reshape(n * 2 * hot_slots, feature)
    hot_embeds = lines_of(pooled, hot_slots, 2 * hot_slots, 0)
    hot_cotan = lines_of(pooled, hot_slots, 2 * hot_slots, hot_slots)
    is_owner = device == hot_expert
    hot_cotan = jnp.where(is_owner, hot_cotan, jnp.zeros_like(hot_cotan))
    own_cotan = jnp.where(flags[:, None], jnp.zeros_like(got_cotan), got_cotan)

    all_embeds = jnp.concatenate([got_embeds, hot_embeds], axis=0)
    all_cotan = jnp.concatenate([own_cotan, hot_cotan], axis=0)
    normed, hidden = trunk(all_embeds, trunk_gain, trunk_weight)
    active, d_gate, d_up, d_rows = through_expert(hidden, all_cotan, gate_w, up_w, down_w)

    share = feature // n
    block = padded(share, TILE // 2)
    column = jnp.arange(n * block, dtype=jnp.int32)
    source = jnp.where(column % block < share, column // block * share + column % block, -1)
    spread = (source[:, None] == jnp.arange(feature, dtype=jnp.int32)[None, :]).astype(
        jnp.bfloat16
    )
    normed_lines = dot_t(spread, normed).astype(jnp.bfloat16)
    grad_trunk = reduce_scatter(normed_lines, d_rows, block, n, experts_axis)[:share]

    grad_gate = t_dot(hidden, d_gate).astype(jnp.bfloat16)[None]
    grad_up = t_dot(hidden, d_up).astype(jnp.bfloat16)[None]
    grad_down = t_dot(active, all_cotan).astype(jnp.bfloat16)[None]
    return (grad_gate, grad_up, grad_down, grad_trunk)


def bit_of(me, bit):
    return (me // (1 << bit)) % 2


def iota(shape, dim):
    return lax.broadcasted_iota(jnp.int32, shape, dim)


def as_ones(mask, kind=jnp.bfloat16):
    return jnp.where(mask, 1.0, 0.0).astype(kind)


def reduce_orders(n, experts_axis):
    bits = n.bit_length() - 1
    core = experts_axis.bit_length() - 1
    others = [b for b in range(bits) if b != core]
    low, high, middle = others[0], others[-1], others[1:-1]
    return [core, high, low] + middle, [core, low, high] + middle


def reduce_widths(width):
    widths = [2 * LANES] * (width // (2 * LANES))
    if width % (2 * LANES):
        widths.append(width % (2 * LANES))
    starts = [sum(widths[:g]) for g in range(len(widths))]
    return list(zip(starts, widths))


def gather_orders(n, experts_axis):
    core, flat, tall, *middle = reduce_orders(n, experts_axis)[0]
    return {EMB: [[middle, [flat], [tall], [core]], [middle, [tall], [flat], [core]], [middle, [flat], [tall], [core]]], COT: [[middle, [flat, tall], [core]], [[flat, tall], middle, [core]], [middle, [flat, tall], [core]]]}


def fused_kernel(n, experts_axis, hot_slots, names, *refs):
    plain, tree = names
    r = types.SimpleNamespace(
        **dict(zip(plain, refs)), **jax.tree.unflatten(tree, refs[len(plain) :])
    )
    bits = n.bit_length() - 1
    tokens, feature = r.emb.shape
    hidden_units = r.wg.shape[1]
    capacity = tokens // n
    hot_rows = n * hot_slots
    share = feature // n
    me = flat_index(experts_axis)
    core = experts_axis.bit_length() - 1
    gather_groups = column_groups(feature)
    gather_plans = gather_orders(n, experts_axis)
    reduce_groups = reduce_widths(feature)
    orders = reduce_orders(n, experts_axis)
    layout = orders[0]

    barrier = pltpu.get_barrier_semaphore()

    def greet(step, carry):
        pl.semaphore_signal(
            barrier,
            inc=1,
            device_id=place(lax.rem(me + step, n), experts_axis),
            device_id_type=MESH,
        )
        return carry

    pairs = (
        (r.tags_hbm, r.tags),
        (r.plan_hbm, r.plan),
        (r.helper_hbm, r.helper),
        (r.emb_hbm, r.emb),
        (r.cot_hbm, r.cot),
        (r.gain_hbm, r.gain),
        (r.tw_hbm, r.tw),
        (r.wg_hbm.at[0], r.wg),
        (r.wu_hbm.at[0], r.wu),
        (r.wd_hbm.at[0], r.wd),
    )
    loads = [
        pltpu.make_async_copy(far, near, r.load_sem.at[index])
        for index, (far, near) in enumerate(pairs)
    ]
    for load in loads[:4]:
        load.start()
    lax.fori_loop(1, n, greet, 0)
    for load in loads[4:]:
        load.start()
    for load in loads[:3]:
        load.wait()

    helper = r.helper[...]
    popular = r.plan[0:1, 0:1]
    foreign = (r.tags[...] == popular) & (helper != popular)
    to_device = iota((n, tokens), 0) == helper
    ahead = as_ones(iota((tokens, tokens), 0) < iota((tokens, tokens), 1))
    to_ones = as_ones(to_device)
    count = jnp.dot(to_ones, ahead, preferred_element_type=jnp.float32)
    slot = jnp.sum(jnp.where(to_device, count, 0.0), axis=0, keepdims=True).astype(jnp.int32)
    target = helper * capacity + slot
    pick = as_ones(iota((tokens, tokens), 0) == target)
    marked = as_ones((iota((LANES, tokens), 0) == slot) & foreign)
    marks = dot_t(to_ones, marked)
    for device in range(n):
        r.out[MARK][device] = marks[device : device + 1]

    def packed(whole):
        rows = jnp.dot(pick, whole[...], preferred_element_type=jnp.float32)
        return rows.reshape(n, capacity, feature).astype(jnp.bfloat16)

    loads[3].wait()
    r.out[EMB][...] = packed(r.emb)

    def exchange_copy(kind, step, arriving):
        other = lax.rem(me + step, n)
        return pltpu.make_async_remote_copy(
            src_ref=r.out[kind].at[other],
            dst_ref=r.into[kind].at[other if arriving else me],
            send_sem=r.send_sem.at[kind, other],
            recv_sem=r.recv_sem.at[kind, other if arriving else me],
            device_id=place(other, experts_axis),
            device_id_type=MESH,
        )

    def start_kinds(first, last, *some):
        def start(step, carry):
            for kind in some:
                exchange_copy(kind, step, False).start()
            return carry

        lax.fori_loop(first, last, start, 0)

    def start_batch(batch):
        parts = len(gather_plans[EMB][0]) + 1
        cuts = [1 + (n - 1) * at // parts for at in range(parts + 1)]
        start_kinds(cuts[batch], cuts[batch + 1], COT)

    def finish_kind(kind):
        def finish(step, carry):
            copy = exchange_copy(kind, step, True)
            copy.wait_send()
            copy.wait_recv()
            return carry

        lax.fori_loop(1, n, finish, 0)

    own = [
        pltpu.make_async_copy(r.out[kind].at[me], r.into[kind].at[me], r.own_sem.at[kind])
        for kind in (MARK, EMB, COT)
    ]

    pl.semaphore_wait(barrier, n - 1)
    start_kinds(1, n, MARK, EMB)
    own[MARK].start()
    own[EMB].start()
    loads[4].wait()
    r.out[COT][...] = packed(r.cot)
    start_batch(0)
    own[COT].start()

    place_row = iota((feature, 1), 0)
    block = jnp.floor((place_row.astype(jnp.float32) + 0.5) / share).astype(jnp.int32)
    source = place_row - block * share
    for position, bit in enumerate(layout):
        part = jnp.right_shift(block, bits - 1 - position) & 1
        source = source + part * (share << bit)
    r.order[...] = as_ones(source == iota((feature, feature), 1))

    def gather_copies(kind, stage):
        copies = []
        for group in range(len(gather_groups)):
            steps = gather_plans[kind][group]
            held = r.held[kind - EMB][group]
            size = 1 << sum(len(step) for step in steps[:stage])
            for mask in range(1, 1 << len(steps[stage])):
                other = me
                for position, bit in enumerate(steps[stage]):
                    if (mask >> position) & 1:
                        other = flipped(other, bit)
                copies.append(
                    pltpu.make_async_remote_copy(
                        src_ref=held.at[pl.ds(0, size)],
                        dst_ref=held.at[pl.ds(mask * size, size)],
                        send_sem=r.gather_send.at[kind - EMB, stage, group, mask],
                        recv_sem=r.gather_recv.at[kind - EMB, stage, group, mask],
                        device_id=place(other, experts_axis),
                        device_id_type=MESH,
                    )
                )
        return copies

    def gather_begin(kind, rows):
        for group, (first, wide) in enumerate(gather_groups):
            r.held[kind - EMB][group][0] = rows[:, first : first + wide].astype(jnp.bfloat16)
        for copy in gather_copies(kind, 0):
            copy.start()

    def gather_step(kind, stage):
        for copy in gather_copies(kind, stage):
            copy.wait()
        if stage + 1 < len(gather_plans[kind][0]):
            for copy in gather_copies(kind, stage + 1):
                copy.start()

    def gathered(kind, group):
        plan = sum(gather_plans[kind][group], [])
        held = r.held[kind - EMB][group]
        parts = []
        for offset in range(n):
            at = sum(1 << position for position in range(bits) if (offset >> plan[position]) & 1)
            parts.append(held[at].astype(jnp.float32))
        return jnp.concatenate(parts, axis=0)

    def unpacked(kind):
        return r.into[kind][...].astype(jnp.float32).reshape(tokens, feature)

    def trunk_rows(values, first, rows):
        factor = lax.rsqrt(jnp.mean(values * values, axis=1, keepdims=True) + 1e-06)
        normed = (values * factor * r.gain[...].reshape(1, feature)).astype(jnp.bfloat16)
        hidden = values + jnp.dot(normed, r.tw[...], preferred_element_type=jnp.float32)
        r.hidden[first : first + rows, :] = hidden.astype(jnp.bfloat16)
        r.normed[:, first : first + rows] = dot_t(r.order[...], normed).astype(
            jnp.bfloat16
        )

    def forward_rows(first, rows):
        hidden = r.hidden[first : first + rows, :]
        r.gate[first : first + rows, :] = jnp.dot(
            hidden, r.wg[...], preferred_element_type=jnp.float32
        )
        r.up[first : first + rows, :] = jnp.dot(
            hidden, r.wu[...], preferred_element_type=jnp.float32
        )

    def backward_rows(first, rows):
        d_active = dot_t(r.cotan[first : first + rows, :], r.wd[...])
        gate_pre = r.gate[first : first + rows, :]
        up_pre = r.up[first : first + rows, :]
        sigma = jax.nn.sigmoid(gate_pre)
        silu_val = gate_pre * sigma
        r.active[first : first + rows, :] = (silu_val * up_pre).astype(jnp.bfloat16)
        r.d_gate[first : first + rows, :] = (
            d_active * up_pre * sigma * (1.0 + gate_pre * (1.0 - sigma))
        ).astype(jnp.bfloat16)
        r.d_up[first : first + rows, :] = (d_active * silu_val).astype(jnp.bfloat16)

    def rows_back(first, rows, column, wide):
        r.d_rows[first : first + rows, column : column + wide] = (
            dot_t(r.d_gate[first : first + rows, :], r.wg[column : column + wide, :])
            + dot_t(r.d_up[first : first + rows, :], r.wu[column : column + wide, :])
        ).astype(jnp.bfloat16)

    side = bit_of(me, core)
    half = feature // 2

    def product(group, which, first, rows):
        column, wide = reduce_groups[group]
        return jnp.dot(
            r.normed[
                pl.ds(pl.multiple_of(which * half, half & -half), half), first : first + rows
            ],
            r.d_rows[first : first + rows, column : column + wide],
            preferred_element_type=jnp.float32,
        )

    groups = range(len(reduce_groups))

    for load in loads[5:]:
        load.wait()
    own[MARK].wait()
    own[EMB].wait()
    finish_kind(MARK)
    finish_kind(EMB)

    by_source = as_ones(
        jnp.floor((iota((tokens, n), 0).astype(jnp.float32) + 0.5) / capacity).astype(jnp.int32)
        == iota((tokens, n), 1)
    )
    marks_in = jnp.concatenate([r.into[MARK][device] for device in range(n)], axis=0)
    spread = jnp.dot(by_source, marks_in.astype(jnp.bfloat16), preferred_element_type=jnp.float32)
    lane = iota((tokens, LANES), 1)
    within = iota((tokens, LANES), 0) & (capacity - 1)
    flag = jnp.sum(jnp.where(lane == within, spread, 0.0), axis=1, keepdims=True)
    before = as_ones(iota((tokens, tokens), 1) < iota((tokens, tokens), 0))
    flag_wide = jnp.broadcast_to(flag, (tokens, LANES))
    rank = jnp.dot(before, flag_wide.astype(jnp.bfloat16), preferred_element_type=jnp.float32)
    chosen = jnp.where(rank.astype(jnp.int32) == lane, flag_wide, 0.0)
    chooser = chosen.T[:hot_slots].astype(jnp.bfloat16)

    got = unpacked(EMB)
    gather_begin(EMB, jnp.dot(chooser, got.astype(jnp.bfloat16), preferred_element_type=jnp.float32))
    start_batch(1)
    trunk_rows(got, 0, tokens)
    for stage in range(len(gather_plans[EMB][0])):
        gather_step(EMB, stage)
        if stage + 1 < len(gather_plans[EMB][0]):
            start_batch(stage + 2)
        if stage == 0:
            forward_rows(0, tokens)

    hot = jnp.concatenate([gathered(EMB, group) for group in range(len(gather_groups))], axis=1)
    trunk_rows(hot, tokens, hot_rows)
    forward_rows(tokens, hot_rows)

    own[COT].wait()
    finish_kind(COT)
    got = unpacked(COT)
    gather_begin(COT, jnp.dot(chooser, got.astype(jnp.bfloat16), preferred_element_type=jnp.float32))
    r.cotan[0:tokens, :] = jnp.where(flag > 0, 0.0, got).astype(jnp.bfloat16)
    backward_rows(0, tokens)
    gather_step(COT, 0)
    rows_back(0, tokens, 0, feature)
    for group in groups:
        r.ahead[group][...] = product(group, 1 - side, 0, tokens)
    gather_step(COT, 1)
    for group in groups:
        r.kept[0][group][...] = product(group, side, 0, tokens)
    for stage in range(2, len(gather_plans[COT][0])):
        gather_step(COT, stage)
    is_owner = popular == me
    for group, (column, wide) in enumerate(gather_groups):
        r.cotan[tokens : tokens + hot_rows, column : column + wide] = jnp.where(
            is_owner, gathered(COT, group), 0.0
        ).astype(jnp.bfloat16)
    backward_rows(tokens, hot_rows)

    def reduce_copy(stage, group):
        bit = orders[group % 2][stage]
        return pltpu.make_async_remote_copy(
            src_ref=r.sent[stage][group],
            dst_ref=r.came[stage][group],
            send_sem=r.reduce_send.at[stage, group],
            recv_sem=r.reduce_recv.at[stage, group],
            device_id=place(flipped(me, bit), experts_axis),
            device_id_type=MESH,
        )

    def pieces(stage, group, side):
        size = feature >> (stage + 1)
        bit = orders[group % 2][stage]
        if stage == 1 and bit != layout[1]:
            step = size // 2
            return [(pl.multiple_of(part * size + side * step, 16), part * step, step) for part in range(2)]
        return [(pl.multiple_of(side * size, size & -size), 0, size)]

    def reduce_step(stage, group):
        side = bit_of(me, orders[group % 2][stage])
        kept, came = r.kept[stage - 1][group], r.came[stage - 1][group]
        size = feature >> (stage + 1)
        reduce_copy(stage - 1, group).wait()
        if size % TILE:
            total = kept[0 : 2 * size] + came[0 : 2 * size].astype(jnp.float32)
            first, second = total[:size], total[size:]
            r.sent[stage][group][0:size] = jnp.where(side == 1, first, second).astype(
                jnp.bfloat16
            )
            reduce_copy(stage, group).start()
            r.kept[stage][group][0:size] = jnp.where(side == 1, second, first)
            return
        for at, into, rows in pieces(stage, group, 1 - side):
            r.sent[stage][group][into : into + rows] = (
                kept[pl.ds(at, rows)] + came[pl.ds(at, rows)].astype(jnp.float32)
            ).astype(jnp.bfloat16)
        reduce_copy(stage, group).start()
        for at, into, rows in pieces(stage, group, side):
            r.kept[stage][group][into : into + rows] = kept[pl.ds(at, rows)] + came[
                pl.ds(at, rows)
            ].astype(jnp.float32)

    work = []
    for into, left, right in (
        (r.grad_gate, r.hidden, r.d_gate),
        (r.grad_up, r.hidden, r.d_up),
        (r.grad_down, r.active, r.cotan),
    ):
        lines = into.shape[1]
        for at, wide in reduce_widths(lines):

            def one(into=into, left=left, right=right, at=at, wide=wide):
                into[0, at : at + wide, :] = t_dot(
                    left[:, at : at + wide], right[...]
                ).astype(jnp.bfloat16)

            work.append(one)
    rows_back(tokens, hot_rows, 0, feature)

    def first_step(group):
        r.sent[0][group][...] = (
            r.ahead[group][...] + product(group, 1 - side, tokens, hot_rows)
        ).astype(jnp.bfloat16)
        reduce_copy(0, group).start()
        r.kept[0][group][...] += product(group, side, tokens, hot_rows)

    steps = sorted(
        ((stage, group) for stage in range(bits) for group in groups),
        key=lambda step: (step[1] + WAVE * step[0], -step[0]),
    )
    done = 0
    later = len(reduce_groups) + 1
    for index, (stage, group) in enumerate(steps):
        if stage == 0:
            first_step(group)
        else:
            reduce_step(stage, group)
        while done * (len(steps) - later) < len(work) * (index + 1 - later):
            work[done]()
            done += 1
    for group in groups:
        column, wide = reduce_groups[group]
        reduce_copy(bits - 1, group).wait()
        r.grad_trunk[:, column : column + wide] = r.kept[bits - 1][group][
            0:share
        ] + r.came[bits - 1][group][0:share].astype(jnp.float32)


def fused_plan(n, hot_slots, tokens, feature, units):
    bits = n.bit_length() - 1
    rows = tokens + n * hot_slots
    capacity = tokens // n
    groups = reduce_widths(feature)
    bf, f32 = jnp.bfloat16, jnp.float32
    message = pltpu.VMEM((n, capacity, feature), bf)
    mark = pltpu.VMEM((n, 1, LANES), f32)

    def stages(kind):
        sizes = [feature >> (stage + 1) for stage in range(bits)]
        return [
            [pltpu.VMEM((padded(size, TILE // 2), wide), kind) for _, wide in groups]
            for size in sizes
        ]

    return dict(
        tags=pltpu.VMEM((1, tokens), jnp.int32),
        plan=pltpu.VMEM((1, n), jnp.int32),
        helper=pltpu.VMEM((1, tokens), jnp.int32),
        gain=pltpu.VMEM((feature,), f32),
        emb=pltpu.VMEM((tokens, feature), bf),
        cot=pltpu.VMEM((tokens, feature), bf),
        tw=pltpu.VMEM((feature, feature), bf),
        wg=pltpu.VMEM((feature, units), bf),
        wu=pltpu.VMEM((feature, units), bf),
        wd=pltpu.VMEM((units, feature), bf),
        out=[mark, message, message],
        into=[mark, message, message],
        order=pltpu.VMEM((feature, feature), bf),
        hidden=pltpu.VMEM((rows, feature), bf),
        normed=pltpu.VMEM((feature, rows), bf),
        cotan=pltpu.VMEM((rows, feature), bf),
        gate=pltpu.VMEM((rows, units), f32),
        up=pltpu.VMEM((rows, units), f32),
        active=pltpu.VMEM((rows, units), bf),
        d_gate=pltpu.VMEM((rows, units), bf),
        d_up=pltpu.VMEM((rows, units), bf),
        d_rows=pltpu.VMEM((rows, feature), bf),
        held=[
            [pltpu.VMEM((n, hot_slots, wide), bf) for _, wide in column_groups(feature)]
            for _ in (EMB, COT)
        ],
        kept=stages(f32),
        ahead=stages(f32)[0],
        sent=stages(bf),
        came=stages(bf),
        load_sem=pltpu.SemaphoreType.DMA((10,)),
        own_sem=pltpu.SemaphoreType.DMA((3,)),
        send_sem=pltpu.SemaphoreType.DMA((3, n)),
        recv_sem=pltpu.SemaphoreType.DMA((3, n)),
        gather_send=pltpu.SemaphoreType.DMA((2, bits, 3, 4)),
        gather_recv=pltpu.SemaphoreType.DMA((2, bits, 3, 4)),
        reduce_send=pltpu.SemaphoreType.DMA((bits, len(groups))),
        reduce_recv=pltpu.SemaphoreType.DMA((bits, len(groups))),
    )


def plan_bytes(plan):
    total = 0
    for item in jax.tree.leaves(plan):
        if len(item.shape) > 1 and item.shape[-1] % LANES == 0:
            lead = 1
            for size in item.shape[:-2]:
                lead *= size
            lines = padded(item.shape[-2], TILE // 2)
            total += lead * lines * item.shape[-1] * jnp.dtype(item.dtype).itemsize
    return total


def settle_kernel(count, *refs):
    sems = refs[-1]
    copies = [
        pltpu.make_async_copy(refs[at], refs[count + at], sems.at[at]) for at in range(count)
    ]
    for copy in copies:
        copy.start()
    for copy in copies:
        copy.wait()


def settle(arrays):
    return pl.pallas_call(
        functools.partial(settle_kernel, len(arrays)),
        out_shape=tuple(jax.ShapeDtypeStruct(array.shape, array.dtype) for array in arrays),
        in_specs=[pl.BlockSpec(memory_space=pl.ANY)] * len(arrays),
        out_specs=(pl.BlockSpec(memory_space=pltpu.HBM),) * len(arrays),
        scratch_shapes=[pltpu.SemaphoreType.DMA((len(arrays),))],
        compiler_params=pltpu.CompilerParams(vmem_limit_bytes=1024 * 1024),
    )(*arrays)


def fused_body(embeds, trunk_gain, trunk_weight, w_gate, w_up, w_down, tags, plan, helper, cotangent):
    n = lax.axis_size(("dp", "expert"))
    experts_axis = lax.axis_size("expert")
    tokens, feature = embeds.shape
    units = w_gate.shape[2]
    hot_slots = tokens // 32
    anywhere = pl.BlockSpec(memory_space=pltpu.HBM)
    inside = pl.BlockSpec(memory_space=pltpu.VMEM)
    inputs = dict(
        emb_hbm=(embeds, anywhere),
        gain_hbm=(trunk_gain, anywhere),
        tw_hbm=(trunk_weight, anywhere),
        wg_hbm=(w_gate, anywhere),
        wu_hbm=(w_up, anywhere),
        wd_hbm=(w_down, anywhere),
        tags_hbm=(tags.reshape(1, tokens), anywhere),
        plan_hbm=(plan.reshape(1, -1), anywhere),
        helper_hbm=(helper.reshape(1, tokens), anywhere),
        cot_hbm=(cotangent, anywhere),
    )
    outputs = dict(
        grad_gate=jax.ShapeDtypeStruct(w_gate.shape, jnp.bfloat16),
        grad_up=jax.ShapeDtypeStruct(w_up.shape, jnp.bfloat16),
        grad_down=jax.ShapeDtypeStruct(w_down.shape, jnp.bfloat16),
        grad_trunk=jax.ShapeDtypeStruct((feature // n, feature), jnp.float32),
    )
    scratch = fused_plan(n, hot_slots, tokens, feature, units)
    names = (list(inputs) + list(outputs), jax.tree.structure(scratch))
    results = pl.pallas_call(
        functools.partial(fused_kernel, n, experts_axis, hot_slots, names),
        out_shape=tuple(outputs.values()),
        in_specs=[spec for _, spec in inputs.values()],
        out_specs=(inside,) * len(outputs),
        scratch_shapes=jax.tree.leaves(scratch),
        compiler_params=pltpu.CompilerParams(
            collective_id=0, has_side_effects=True, vmem_limit_bytes=VMEM_BYTES
        ),
    )(*[pltpu.with_memory_space_constraint(value, pltpu.HBM) for value, _ in inputs.values()])
    return settle(results)


def fits(embeds, w_gate, n):
    tokens, feature = embeds.shape
    units = w_gate.shape[2]
    hot_slots = tokens // 32
    if (tokens // n) % 8 or hot_slots % 8 or feature % (16 * n // 4):
        return False
    return plan_bytes(fused_plan(n, hot_slots, tokens, feature, units)) < VMEM_BYTES - 2 * 1024 * 1024


def either(*args):
    n = lax.axis_size(("dp", "expert"))
    return (fused_body if fits(args[0], args[3], n) else body)(*args)


def solution(mesh):
    spread_rows = P(("dp", "expert"), None)
    spread_first = P(("dp", "expert"), None, None)
    return jax.shard_map(
        either,
        mesh=mesh,
        in_specs=(
            spread_rows,
            P(),
            P(),
            spread_first,
            spread_first,
            spread_first,
            P(("dp", "expert")),
            P(),
            P(("dp", "expert")),
            spread_rows,
        ),
        out_specs=(spread_first, spread_first, spread_first, spread_rows),
        check_vma=False,
    )
```

```python
import functools
import types

import jax
import jax.numpy as jnp
from jax import lax
from jax.experimental import pallas as pl
from jax.experimental.pallas import tpu as pltpu
from jax.sharding import PartitionSpec as P

LANES = 128
TILE = 16
MESH = pl.DeviceIdType.MESH
MARK, EMB, COT = range(3)
WAVE = 99
VMEM_BYTES = 45 * 1024 * 1024


def padded(value, multiple):
    return -(-value // multiple) * multiple


def flat_index(experts_axis):
    return lax.axis_index("dp") * experts_axis + lax.axis_index("expert")


def place(flat, experts_axis):
    return (flat // experts_axis, flat % experts_axis)


def flipped(me, bit):
    weight = 1 << bit
    return me + (1 - 2 * ((me // weight) % 2)) * weight


def greet_all(n, experts_axis):
    me = flat_index(experts_axis)
    barrier = pltpu.get_barrier_semaphore()

    def greet(step, carry):
        pl.semaphore_signal(
            barrier,
            inc=1,
            device_id=place(lax.rem(me + step, n), experts_axis),
            device_id_type=MESH,
        )
        return carry

    lax.fori_loop(1, n, greet, 0)
    pl.semaphore_wait(barrier, n - 1)


def greet_bits(bits, experts_axis):
    me = flat_index(experts_axis)
    barrier = pltpu.get_barrier_semaphore()
    for bit in range(bits):
        pl.semaphore_signal(
            barrier, inc=1, device_id=place(flipped(me, bit), experts_axis), device_id_type=MESH
        )
    pl.semaphore_wait(barrier, bits)


def exchange_kernel(n, experts_axis, send_ref, out_ref, send_sem, recv_sem, own_sem):
    me = flat_index(experts_axis)
    greet_all(n, experts_axis)
    own = pltpu.make_async_copy(send_ref.at[me], out_ref.at[me], own_sem)
    own.start()

    def copy_to(step):
        to = lax.rem(me + step, n)
        return pltpu.make_async_remote_copy(
            src_ref=send_ref.at[to],
            dst_ref=out_ref.at[me],
            send_sem=send_sem.at[to],
            recv_sem=recv_sem.at[me],
            device_id=place(to, experts_axis),
            device_id_type=MESH,
        )

    def copy_from(step):
        source = lax.rem(me + step, n)
        return pltpu.make_async_remote_copy(
            src_ref=send_ref.at[source],
            dst_ref=out_ref.at[source],
            send_sem=send_sem.at[source],
            recv_sem=recv_sem.at[source],
            device_id=place(source, experts_axis),
            device_id_type=MESH,
        )

    def start(step, carry):
        copy_to(step).start()
        return carry

    def finish(step, carry):
        copy = copy_from(step)
        copy.wait_send()
        copy.wait_recv()
        return carry

    lax.fori_loop(1, n, start, 0)
    own.wait()
    lax.fori_loop(1, n, finish, 0)


def exchange(send, n, experts_axis):
    return pl.pallas_call(
        functools.partial(exchange_kernel, n, experts_axis),
        out_shape=jax.ShapeDtypeStruct(send.shape, send.dtype),
        in_specs=[pl.BlockSpec(memory_space=pltpu.VMEM)],
        out_specs=pl.BlockSpec(memory_space=pltpu.VMEM),
        scratch_shapes=[
            pltpu.SemaphoreType.DMA((n,)),
            pltpu.SemaphoreType.DMA((n,)),
            pltpu.SemaphoreType.DMA,
        ],
        compiler_params=pltpu.CompilerParams(
            collective_id=0, has_side_effects=True, vmem_limit_bytes=40 * 1024 * 1024
        ),
    )(send)


def axis_orders(n, experts_axis):
    bits = n.bit_length() - 1
    core = experts_axis.bit_length() - 1
    others = [b for b in range(bits) if b != core]
    low = others[0]
    high = others[-1]
    middle = others[1:-1]
    return core, [
        [high, low] + middle,
        [low] + middle + [high],
        middle + [high, low],
    ]


def column_groups(width):
    tiles = width // LANES
    cuts = [(tiles * g) // 3 * LANES for g in range(4)]
    return [(cuts[g], cuts[g + 1] - cuts[g]) for g in range(3)]


def gather_kernel(n, experts_axis, width, mine_ref, out_ref, *scratch):
    bits = n.bit_length() - 1
    me = flat_index(experts_axis)
    core, orders = axis_orders(n, experts_axis)
    held, send_sem, recv_sem = scratch[:3], scratch[3], scratch[4]
    for group, (first, wide) in enumerate(column_groups(width)):
        held[group][0] = mine_ref[:, first : first + wide]
    greet_bits(bits, experts_axis)
    plans = [order[::-1] + [core] for order in orders]
    for stage in range(bits):
        count = 1 << stage
        copies = []
        for group in range(3):
            bit = plans[group][stage]
            copy = pltpu.make_async_remote_copy(
                src_ref=held[group].at[pl.ds(0, count)],
                dst_ref=held[group].at[pl.ds(count, count)],
                send_sem=send_sem.at[stage, group],
                recv_sem=recv_sem.at[stage, group],
                device_id=place(flipped(me, bit), experts_axis),
                device_id_type=MESH,
            )
            copy.start()
            copies.append(copy)
        for copy in copies:
            copy.wait()
    for group, (first, wide) in enumerate(column_groups(width)):
        for slot in range(n):
            offset = sum(
                1 << plans[group][stage] for stage in range(bits) if (slot >> stage) & 1
            )
            out_ref[offset, :, first : first + wide] = held[group][slot]


def gather(mine, n, experts_axis):
    rows, width = mine.shape
    bits = n.bit_length() - 1
    return pl.pallas_call(
        functools.partial(gather_kernel, n, experts_axis, width),
        out_shape=jax.ShapeDtypeStruct((n, rows, width), mine.dtype),
        in_specs=[pl.BlockSpec(memory_space=pltpu.VMEM)],
        out_specs=pl.BlockSpec(memory_space=pltpu.VMEM),
        scratch_shapes=[
            pltpu.VMEM((n, rows, wide), mine.dtype) for _, wide in column_groups(width)
        ]
        + [pltpu.SemaphoreType.DMA((bits, 3)), pltpu.SemaphoreType.DMA((bits, 3))],
        compiler_params=pltpu.CompilerParams(
            collective_id=1, has_side_effects=True, vmem_limit_bytes=48 * 1024 * 1024
        ),
    )(mine)


def stage_types(bits):
    return [jnp.bfloat16 if stage < 3 else jnp.float32 for stage in range(bits)]


def reduce_kernel(n, experts_axis, block, width, left_ref, right_ref, out_ref, *scratch):
    bits = n.bit_length() - 1
    me = flat_index(experts_axis)
    core, orders = axis_orders(n, experts_axis)
    plans = [[core] + order for order in orders]
    groups = column_groups(width)
    types = stage_types(bits)
    kept = [[scratch[3 * (s * 3 + g)] for g in range(3)] for s in range(bits)]
    sent = [[scratch[3 * (s * 3 + g) + 1] for g in range(3)] for s in range(bits)]
    came = [[scratch[3 * (s * 3 + g) + 2] for g in range(3)] for s in range(bits)]
    send_sem, recv_sem = scratch[9 * bits], scratch[9 * bits + 1]
    greet_bits(bits, experts_axis)

    def transfer(stage, group):
        return pltpu.make_async_remote_copy(
            src_ref=sent[stage][group],
            dst_ref=came[stage][group],
            send_sem=send_sem.at[stage, group],
            recv_sem=recv_sem.at[stage, group],
            device_id=place(flipped(me, plans[group][stage]), experts_axis),
            device_id_type=MESH,
        )

    def side_of(bit):
        return (me // (1 << bit)) % 2

    chunk = experts_axis * block
    spans = n // (2 * experts_axis)

    def first_half(group, side, into, kind):
        first, wide = groups[group]
        for span in range(spans):
            at = pl.multiple_of((2 * span + side) * chunk, chunk)
            product = jnp.dot(
                left_ref[pl.ds(at, chunk), :],
                right_ref[:, first : first + wide],
                preferred_element_type=jnp.float32,
            )
            for item in range(experts_axis):
                into[span * experts_axis + item] = product[
                    item * block : (item + 1) * block
                ].astype(kind)

    for group in range(3):
        first_half(group, 1 - side_of(core), sent[0][group], types[0])
        transfer(0, group).start()
    for group in range(3):
        first_half(group, side_of(core), kept[0][group], jnp.float32)

    left = [[b for b in range(bits - 1, -1, -1) if b != core] for _ in groups]
    for stage in range(1, bits):
        half = n >> (stage + 1)
        for group in range(3):
            bit = plans[group][stage]
            low = 1 << (len(left[group]) - left[group].index(bit) - 1)
            left[group].remove(bit)
            mine = side_of(bit)

            def move(side, into, kind, low=low, stage=stage, group=group, half=half):
                def one(item, carry):
                    at = (item // low) * (2 * low) + side * low + item % low
                    into[item] = (
                        kept[stage - 1][group][at]
                        + came[stage - 1][group][at].astype(jnp.float32)
                    ).astype(kind)
                    return carry

                lax.fori_loop(0, half, one, 0)

            transfer(stage - 1, group).wait()
            move(1 - mine, sent[stage][group], types[stage])
            transfer(stage, group).start()
            move(mine, kept[stage][group], jnp.float32)
    for group, (first, wide) in enumerate(groups):
        transfer(bits - 1, group).wait()
        out_ref[:, first : first + wide] = kept[bits - 1][group][0] + came[bits - 1][group][
            0
        ].astype(jnp.float32)


def reduce_scatter(left, right, block, n, experts_axis):
    width = right.shape[1]
    bits = n.bit_length() - 1
    types = stage_types(bits)
    scratch = []
    for stage in range(bits):
        half = n >> (stage + 1)
        for _, wide in column_groups(width):
            scratch.append(pltpu.VMEM((half, block, wide), jnp.float32))
            scratch.append(pltpu.VMEM((half, block, wide), types[stage]))
            scratch.append(pltpu.VMEM((half, block, wide), types[stage]))
    return pl.pallas_call(
        functools.partial(reduce_kernel, n, experts_axis, block, width),
        out_shape=jax.ShapeDtypeStruct((block, width), jnp.float32),
        in_specs=[pl.BlockSpec(memory_space=pltpu.VMEM)] * 2,
        out_specs=pl.BlockSpec(memory_space=pltpu.VMEM),
        scratch_shapes=scratch
        + [pltpu.SemaphoreType.DMA((bits, 3)), pltpu.SemaphoreType.DMA((bits, 3))],
        compiler_params=pltpu.CompilerParams(
            collective_id=2, has_side_effects=True, vmem_limit_bytes=52 * 1024 * 1024
        ),
    )(left, right)


def lines_of(blocks, count, rows, first):
    lines = blocks.shape[0]
    wanted = jnp.arange(lines // rows * count, dtype=jnp.int32)
    wanted = wanted // count * rows + first + wanted % count
    chosen = wanted[:, None] == jnp.arange(lines, dtype=jnp.int32)[None, :]
    return jnp.dot(
        chosen.astype(jnp.bfloat16), blocks, preferred_element_type=jnp.float32
    ).astype(jnp.bfloat16)


def trunk(rows, gain, weight):
    values = rows.astype(jnp.float32)
    factor = lax.rsqrt(jnp.mean(values * values, axis=1, keepdims=True) + 1e-06)
    normed = (values * factor * gain).astype(jnp.bfloat16)
    hidden = values + jnp.dot(normed, weight, preferred_element_type=jnp.float32)
    return normed, hidden.astype(jnp.bfloat16)


def dot_t(a, b):
    return lax.dot_general(a, b, (((1,), (1,)), ((), ())), preferred_element_type=jnp.float32)


def t_dot(a, b):
    return lax.dot_general(a, b, (((0,), (0,)), ((), ())), preferred_element_type=jnp.float32)


def through_expert(hidden, cotan, gate_w, up_w, down_w):
    gate_pre = jnp.dot(hidden, gate_w, preferred_element_type=jnp.float32)
    up_pre = jnp.dot(hidden, up_w, preferred_element_type=jnp.float32)
    sigma = jax.nn.sigmoid(gate_pre)
    silu_val = gate_pre * sigma
    active = (silu_val * up_pre).astype(jnp.bfloat16)
    d_active = dot_t(cotan, down_w)
    d_gate = (d_active * up_pre * sigma * (1.0 + gate_pre * (1.0 - sigma))).astype(jnp.bfloat16)
    d_up = (d_active * silu_val).astype(jnp.bfloat16)
    d_rows = (dot_t(d_gate, gate_w) + dot_t(d_up, up_w)).astype(jnp.bfloat16)
    return active, d_gate, d_up, d_rows


def body(embeds, trunk_gain, trunk_weight, w_gate, w_up, w_down, tags, plan, helper, cotangent):
    n = lax.axis_size(("dp", "expert"))
    experts_axis = lax.axis_size("expert")
    device = flat_index(experts_axis)
    hot_expert = plan[0]
    tokens, feature = embeds.shape
    capacity = tokens // n
    hot_slots = tokens // 32
    rows = padded(2 * capacity, TILE)
    gate_w, up_w, down_w = w_gate[0], w_up[0], w_down[0]

    token = jnp.arange(tokens, dtype=jnp.int32)
    before = (helper[:, None] == helper[None, :]) & (token[:, None] > token[None, :])
    slot = jnp.sum(before.astype(jnp.int32), axis=1)
    target = helper * rows + slot
    line = jnp.arange(n * rows, dtype=jnp.int32)
    pick = jnp.concatenate(
        [line[:, None] == target[None, :], line[:, None] == target[None, :] + capacity], axis=1
    ).astype(jnp.bfloat16)
    flagged = ((tags == hot_expert) & (helper != hot_expert)).astype(jnp.bfloat16)
    flag_lanes = jnp.broadcast_to(flagged[:, None], (tokens, LANES))
    content = jnp.concatenate(
        [
            jnp.concatenate([embeds, flag_lanes], axis=1),
            jnp.concatenate([cotangent, jnp.zeros_like(flag_lanes)], axis=1),
        ],
        axis=0,
    )
    send = jnp.dot(pick, content, preferred_element_type=jnp.float32).astype(jnp.bfloat16)
    got = exchange(send.reshape(n, rows, feature + LANES), n, experts_axis)
    got = got.reshape(n * rows, feature + LANES)
    got_wide = lines_of(got, capacity, rows, 0)
    got_embeds = got_wide[:, :feature]
    got_cotan = lines_of(got[:, :feature], capacity, rows, capacity)
    flags = got_wide[:, feature] > 0

    rank = jnp.sum((flags[None, :] & (token[:, None] > token[None, :])).astype(jnp.int32), axis=1)
    picker = (rank[None, :] == jnp.arange(hot_slots, dtype=jnp.int32)[:, None]) & flags[None, :]
    picker = picker.astype(jnp.bfloat16)
    hot = jnp.concatenate(
        [
            jnp.dot(picker, got_embeds, preferred_element_type=jnp.float32),
            jnp.dot(picker, got_cotan, preferred_element_type=jnp.float32),
        ],
        axis=0,
    ).astype(jnp.bfloat16)
    pooled = gather(hot, n, experts_axis)
    pooled = pooled.reshape(n * 2 * hot_slots, feature)
    hot_embeds = lines_of(pooled, hot_slots, 2 * hot_slots, 0)
    hot_cotan = lines_of(pooled, hot_slots, 2 * hot_slots, hot_slots)
    is_owner = device == hot_expert
    hot_cotan = jnp.where(is_owner, hot_cotan, jnp.zeros_like(hot_cotan))
    own_cotan = jnp.where(flags[:, None], jnp.zeros_like(got_cotan), got_cotan)

    all_embeds = jnp.concatenate([got_embeds, hot_embeds], axis=0)
    all_cotan = jnp.concatenate([own_cotan, hot_cotan], axis=0)
    normed, hidden = trunk(all_embeds, trunk_gain, trunk_weight)
    active, d_gate, d_up, d_rows = through_expert(hidden, all_cotan, gate_w, up_w, down_w)

    share = feature // n
    block = padded(share, TILE // 2)
    column = jnp.arange(n * block, dtype=jnp.int32)
    source = jnp.where(column % block < share, column // block * share + column % block, -1)
    spread = (source[:, None] == jnp.arange(feature, dtype=jnp.int32)[None, :]).astype(
        jnp.bfloat16
    )
    normed_lines = dot_t(spread, normed).astype(jnp.bfloat16)
    grad_trunk = reduce_scatter(normed_lines, d_rows, block, n, experts_axis)[:share]

    grad_gate = t_dot(hidden, d_gate).astype(jnp.bfloat16)[None]
    grad_up = t_dot(hidden, d_up).astype(jnp.bfloat16)[None]
    grad_down = t_dot(active, all_cotan).astype(jnp.bfloat16)[None]
    return (grad_gate, grad_up, grad_down, grad_trunk)


def bit_of(me, bit):
    return (me // (1 << bit)) % 2


def iota(shape, dim):
    return lax.broadcasted_iota(jnp.int32, shape, dim)


def as_ones(mask, kind=jnp.bfloat16):
    return jnp.where(mask, 1.0, 0.0).astype(kind)


def reduce_orders(n, experts_axis):
    bits = n.bit_length() - 1
    core = experts_axis.bit_length() - 1
    others = [b for b in range(bits) if b != core]
    low, high, middle = others[0], others[-1], others[1:-1]
    return [core, high, low] + middle, [core, low, high] + middle


def reduce_widths(width):
    widths = [2 * LANES] * (width // (2 * LANES))
    if width % (2 * LANES):
        widths.append(width % (2 * LANES))
    starts = [sum(widths[:g]) for g in range(len(widths))]
    return list(zip(starts, widths))


def gather_orders(n, experts_axis):
    core, flat, tall, *middle = reduce_orders(n, experts_axis)[0]
    return {EMB: [[middle, [flat], [tall], [core]], [middle, [tall], [flat], [core]], [middle, [flat], [tall], [core]]], COT: [[middle, [flat, tall], [core]], [[flat, tall], middle, [core]], [middle, [flat, tall], [core]]]}


def fused_kernel(n, experts_axis, hot_slots, names, *refs):
    plain, tree = names
    r = types.SimpleNamespace(
        **dict(zip(plain, refs)), **jax.tree.unflatten(tree, refs[len(plain) :])
    )
    bits = n.bit_length() - 1
    tokens, feature = r.emb.shape
    hidden_units = r.wg.shape[1]
    capacity = tokens // n
    hot_rows = n * hot_slots
    share = feature // n
    me = flat_index(experts_axis)
    core = experts_axis.bit_length() - 1
    gather_groups = column_groups(feature)
    gather_plans = gather_orders(n, experts_axis)
    reduce_groups = reduce_widths(feature)
    orders = reduce_orders(n, experts_axis)
    layout = orders[0]
    lasts = 1 << (bits - 3)

    barrier = pltpu.get_barrier_semaphore()

    def greet(step, carry):
        pl.semaphore_signal(
            barrier,
            inc=1,
            device_id=place(lax.rem(me + step, n), experts_axis),
            device_id_type=MESH,
        )
        return carry

    pairs = (
        (r.tags_hbm, r.tags),
        (r.plan_hbm, r.plan),
        (r.helper_hbm, r.helper),
        (r.emb_hbm, r.emb),
        (r.cot_hbm, r.cot),
        (r.gain_hbm, r.gain),
        (r.tw_hbm, r.tw),
        (r.wg_hbm.at[0], r.wg),
        (r.wu_hbm.at[0], r.wu),
        (r.wd_hbm.at[0], r.wd),
    )
    loads = [
        pltpu.make_async_copy(far, near, r.load_sem.at[index])
        for index, (far, near) in enumerate(pairs)
    ]
    for load in loads[:4]:
        load.start()
    lax.fori_loop(1, n, greet, 0)
    for load in loads[4:]:
        load.start()
    for load in loads[:3]:
        load.wait()

    helper = r.helper[...]
    popular = r.plan[0:1, 0:1]
    foreign = (r.tags[...] == popular) & (helper != popular)
    to_device = iota((n, tokens), 0) == helper
    ahead = as_ones(iota((tokens, tokens), 0) < iota((tokens, tokens), 1))
    to_ones = as_ones(to_device)
    count = jnp.dot(to_ones, ahead, preferred_element_type=jnp.float32)
    slot = jnp.sum(jnp.where(to_device, count, 0.0), axis=0, keepdims=True).astype(jnp.int32)
    target = helper * capacity + slot
    pick = as_ones(iota((tokens, tokens), 0) == target)
    marked = as_ones((iota((LANES, tokens), 0) == slot) & foreign)
    marks = dot_t(to_ones, marked)
    for device in range(n):
        r.out[MARK][device] = marks[device : device + 1]

    def packed(whole):
        rows = jnp.dot(pick, whole[...], preferred_element_type=jnp.float32)
        return rows.reshape(n, capacity, feature).astype(jnp.bfloat16)

    loads[3].wait()
    r.out[EMB][...] = packed(r.emb)

    def exchange_copy(kind, step, arriving):
        other = lax.rem(me + step, n)
        return pltpu.make_async_remote_copy(
            src_ref=r.out[kind].at[other],
            dst_ref=r.into[kind].at[other if arriving else me],
            send_sem=r.send_sem.at[kind, other],
            recv_sem=r.recv_sem.at[kind, other if arriving else me],
            device_id=place(other, experts_axis),
            device_id_type=MESH,
        )

    def start_kinds(first, last, *some):
        def start(step, carry):
            for kind in some:
                exchange_copy(kind, step, False).start()
            return carry

        lax.fori_loop(first, last, start, 0)

    def start_batch(batch):
        parts = len(gather_plans[EMB][0]) + 1
        cuts = [1 + (n - 1) * at // parts for at in range(parts + 1)]
        start_kinds(cuts[batch], cuts[batch + 1], COT)

    def finish_kind(kind):
        def finish(step, carry):
            copy = exchange_copy(kind, step, True)
            copy.wait_send()
            copy.wait_recv()
            return carry

        lax.fori_loop(1, n, finish, 0)

    own = [
        pltpu.make_async_copy(r.out[kind].at[me], r.into[kind].at[me], r.own_sem.at[kind])
        for kind in (MARK, EMB, COT)
    ]

    pl.semaphore_wait(barrier, n - 1)
    start_kinds(1, n, MARK, EMB)
    own[MARK].start()
    own[EMB].start()
    loads[4].wait()
    r.out[COT][...] = packed(r.cot)
    start_batch(0)
    own[COT].start()

    place_row = iota((feature, 1), 0)
    block = jnp.floor((place_row.astype(jnp.float32) + 0.5) / share).astype(jnp.int32)
    source = place_row - block * share
    for position, bit in enumerate(layout):
        part = jnp.right_shift(block, bits - 1 - position) & 1
        source = source + part * (share << bit)
    r.order[...] = as_ones(source == iota((feature, feature), 1))

    def gather_copies(kind, stage):
        copies = []
        for group in range(len(gather_groups)):
            steps = gather_plans[kind][group]
            held = r.held[kind - EMB][group]
            size = 1 << sum(len(step) for step in steps[:stage])
            for mask in range(1, 1 << len(steps[stage])):
                other = me
                for position, bit in enumerate(steps[stage]):
                    if (mask >> position) & 1:
                        other = flipped(other, bit)
                copies.append(
                    pltpu.make_async_remote_copy(
                        src_ref=held.at[pl.ds(0, size)],
                        dst_ref=held.at[pl.ds(mask * size, size)],
                        send_sem=r.gather_send.at[kind - EMB, stage, group, mask],
                        recv_sem=r.gather_recv.at[kind - EMB, stage, group, mask],
                        device_id=place(other, experts_axis),
                        device_id_type=MESH,
                    )
                )
        return copies

    def gather_begin(kind, rows):
        for group, (first, wide) in enumerate(gather_groups):
            r.held[kind - EMB][group][0] = rows[:, first : first + wide].astype(jnp.bfloat16)
        for copy in gather_copies(kind, 0):
            copy.start()

    def gather_step(kind, stage):
        for copy in gather_copies(kind, stage):
            copy.wait()
        if stage + 1 < len(gather_plans[kind][0]):
            for copy in gather_copies(kind, stage + 1):
                copy.start()

    def gathered(kind, group):
        plan = sum(gather_plans[kind][group], [])
        held = r.held[kind - EMB][group]
        parts = []
        for offset in range(n):
            at = sum(1 << position for position in range(bits) if (offset >> plan[position]) & 1)
            parts.append(held[at].astype(jnp.float32))
        return jnp.concatenate(parts, axis=0)

    def unpacked(kind):
        return r.into[kind][...].astype(jnp.float32).reshape(tokens, feature)

    def trunk_rows(values, first, rows):
        factor = lax.rsqrt(jnp.mean(values * values, axis=1, keepdims=True) + 1e-06)
        normed = (values * factor * r.gain[...].reshape(1, feature)).astype(jnp.bfloat16)
        hidden = values + jnp.dot(normed, r.tw[...], preferred_element_type=jnp.float32)
        r.hidden[first : first + rows, :] = hidden.astype(jnp.bfloat16)
        r.normed[:, first : first + rows] = dot_t(r.order[...], normed).astype(
            jnp.bfloat16
        )

    def forward_rows(first, rows):
        hidden = r.hidden[first : first + rows, :]
        r.gate[first : first + rows, :] = jnp.dot(
            hidden, r.wg[...], preferred_element_type=jnp.float32
        )
        r.up[first : first + rows, :] = jnp.dot(
            hidden, r.wu[...], preferred_element_type=jnp.float32
        )

    def backward_rows(first, rows):
        d_active = dot_t(r.cotan[first : first + rows, :], r.wd[...])
        gate_pre = r.gate[first : first + rows, :]
        up_pre = r.up[first : first + rows, :]
        sigma = jax.nn.sigmoid(gate_pre)
        silu_val = gate_pre * sigma
        r.active[first : first + rows, :] = (silu_val * up_pre).astype(jnp.bfloat16)
        r.d_gate[first : first + rows, :] = (
            d_active * up_pre * sigma * (1.0 + gate_pre * (1.0 - sigma))
        ).astype(jnp.bfloat16)
        r.d_up[first : first + rows, :] = (d_active * silu_val).astype(jnp.bfloat16)

    def rows_back(first, rows, column, wide):
        r.d_rows[first : first + rows, column : column + wide] = (
            dot_t(r.d_gate[first : first + rows, :], r.wg[column : column + wide, :])
            + dot_t(r.d_up[first : first + rows, :], r.wu[column : column + wide, :])
        ).astype(jnp.bfloat16)

    side = bit_of(me, core)
    half = feature // 2

    def product(group, which, first, rows):
        column, wide = reduce_groups[group]
        return jnp.dot(
            r.normed[
                pl.ds(pl.multiple_of(which * half, half & -half), half), first : first + rows
            ],
            r.d_rows[first : first + rows, column : column + wide],
            preferred_element_type=jnp.float32,
        )

    groups = range(len(reduce_groups))

    for load in loads[5:]:
        load.wait()
    own[MARK].wait()
    own[EMB].wait()
    finish_kind(MARK)
    finish_kind(EMB)

    by_source = as_ones(
        jnp.floor((iota((tokens, n), 0).astype(jnp.float32) + 0.5) / capacity).astype(jnp.int32)
        == iota((tokens, n), 1)
    )
    marks_in = jnp.concatenate([r.into[MARK][device] for device in range(n)], axis=0)
    spread = jnp.dot(by_source, marks_in.astype(jnp.bfloat16), preferred_element_type=jnp.float32)
    lane = iota((tokens, LANES), 1)
    within = iota((tokens, LANES), 0) & (capacity - 1)
    flag = jnp.sum(jnp.where(lane == within, spread, 0.0), axis=1, keepdims=True)
    before = as_ones(iota((tokens, tokens), 1) < iota((tokens, tokens), 0))
    flag_wide = jnp.broadcast_to(flag, (tokens, LANES))
    rank = jnp.dot(before, flag_wide.astype(jnp.bfloat16), preferred_element_type=jnp.float32)
    chosen = jnp.where(rank.astype(jnp.int32) == lane, flag_wide, 0.0)
    chooser = chosen.T[:hot_slots].astype(jnp.bfloat16)

    got = unpacked(EMB)
    gather_begin(EMB, jnp.dot(chooser, got.astype(jnp.bfloat16), preferred_element_type=jnp.float32))
    start_batch(1)
    trunk_rows(got, 0, tokens)
    for stage in range(len(gather_plans[EMB][0])):
        gather_step(EMB, stage)
        if stage + 1 < len(gather_plans[EMB][0]):
            start_batch(stage + 2)
        if stage == 0:
            forward_rows(0, tokens)

    hot = jnp.concatenate([gathered(EMB, group) for group in range(len(gather_groups))], axis=1)
    trunk_rows(hot, tokens, hot_rows)
    forward_rows(tokens, hot_rows)

    own[COT].wait()
    finish_kind(COT)
    got = unpacked(COT)
    gather_begin(COT, jnp.dot(chooser, got.astype(jnp.bfloat16), preferred_element_type=jnp.float32))
    r.cotan[0:tokens, :] = jnp.where(flag > 0, 0.0, got).astype(jnp.bfloat16)
    backward_rows(0, tokens)
    gather_step(COT, 0)
    rows_back(0, tokens, 0, feature)
    for group in groups:
        r.ahead[group][...] = product(group, 1 - side, 0, tokens)
    gather_step(COT, 1)
    for group in groups:
        r.kept[0][group][...] = product(group, side, 0, tokens)
    for stage in range(2, len(gather_plans[COT][0])):
        gather_step(COT, stage)
    is_owner = popular == me
    for group, (column, wide) in enumerate(gather_groups):
        r.cotan[tokens : tokens + hot_rows, column : column + wide] = jnp.where(
            is_owner, gathered(COT, group), 0.0
        ).astype(jnp.bfloat16)
    backward_rows(tokens, hot_rows)

    def reduce_copy(stage, group):
        bit = orders[group % 2][stage]
        return pltpu.make_async_remote_copy(
            src_ref=r.sent[stage][group],
            dst_ref=r.came[stage][group],
            send_sem=r.reduce_send.at[stage, group],
            recv_sem=r.reduce_recv.at[stage, group],
            device_id=place(flipped(me, bit), experts_axis),
            device_id_type=MESH,
        )

    def pieces(stage, group, side):
        size = feature >> (stage + 1)
        bit = orders[group % 2][stage]
        if stage == 1 and bit != layout[1]:
            step = size // 2
            return [(pl.multiple_of(part * size + side * step, 16), part * step, step) for part in range(2)]
        return [(pl.multiple_of(side * size, size & -size), 0, size)]

    def last_copies(group):
        copies = []
        for mask in range(1, lasts):
            other = me
            for position, bit in enumerate(layout[:2:-1]):
                if (mask >> position) & 1:
                    other = flipped(other, bit)
            copies.append(
                pltpu.make_async_remote_copy(
                    src_ref=r.last_out[group].at[mask],
                    dst_ref=r.last_in[group].at[mask],
                    send_sem=r.last_send.at[group, mask],
                    recv_sem=r.last_recv.at[group, mask],
                    device_id=place(other, experts_axis),
                    device_id_type=MESH,
                )
            )
        return copies

    def last_step(group):
        reduce_copy(2, group).wait()
        total = r.kept[2][group][...] + r.came[2][group][...].astype(jnp.float32)
        blocks = [total[at * share : (at + 1) * share] for at in range(lasts)]
        for position, bit in enumerate(layout[:2:-1]):
            swap = bit_of(me, bit) == 1
            blocks = [
                jnp.where(swap, blocks[at ^ (1 << position)], blocks[at]) for at in range(lasts)
            ]
        for mask in range(1, lasts):
            r.last_out[group][mask, 0:share] = blocks[mask].astype(jnp.bfloat16)
        for copy in last_copies(group):
            copy.start()
        r.last_kept[group][0:share] = blocks[0]

    def reduce_step(stage, group):
        side = bit_of(me, orders[group % 2][stage])
        kept, came = r.kept[stage - 1][group], r.came[stage - 1][group]
        size = feature >> (stage + 1)
        reduce_copy(stage - 1, group).wait()
        for at, into, rows in pieces(stage, group, 1 - side):
            r.sent[stage][group][into : into + rows] = (
                kept[pl.ds(at, rows)] + came[pl.ds(at, rows)].astype(jnp.float32)
            ).astype(jnp.bfloat16)
        reduce_copy(stage, group).start()
        for at, into, rows in pieces(stage, group, side):
            r.kept[stage][group][into : into + rows] = kept[pl.ds(at, rows)] + came[
                pl.ds(at, rows)
            ].astype(jnp.float32)

    work = []
    for into, left, right in (
        (r.grad_gate, r.hidden, r.d_gate),
        (r.grad_up, r.hidden, r.d_up),
        (r.grad_down, r.active, r.cotan),
    ):
        lines = into.shape[1]
        for at, wide in reduce_widths(lines):

            def one(into=into, left=left, right=right, at=at, wide=wide):
                into[0, at : at + wide, :] = t_dot(
                    left[:, at : at + wide], right[...]
                ).astype(jnp.bfloat16)

            work.append(one)
    rows_back(tokens, hot_rows, 0, feature)

    def first_step(group):
        r.sent[0][group][...] = (
            r.ahead[group][...] + product(group, 1 - side, tokens, hot_rows)
        ).astype(jnp.bfloat16)
        reduce_copy(0, group).start()
        r.kept[0][group][...] += product(group, side, tokens, hot_rows)

    steps = sorted(
        ((stage, group) for stage in range(4) for group in groups),
        key=lambda step: (step[1] + WAVE * step[0], -step[0]),
    )
    done = 0
    later = len(reduce_groups) + 1
    for index, (stage, group) in enumerate(steps):
        if stage == 0:
            first_step(group)
        elif stage == 3:
            last_step(group)
        else:
            reduce_step(stage, group)
        while done * (len(steps) - later) < len(work) * (index + 1 - later):
            work[done]()
            done += 1
    for group in groups:
        column, wide = reduce_groups[group]
        for copy in last_copies(group):
            copy.wait()
        total = r.last_kept[group][0:share]
        for mask in range(1, lasts):
            total = total + r.last_in[group][mask, 0:share].astype(jnp.float32)
        r.grad_trunk[:, column : column + wide] = total


def fused_plan(n, hot_slots, tokens, feature, units):
    bits = n.bit_length() - 1
    rows = tokens + n * hot_slots
    capacity = tokens // n
    groups = reduce_widths(feature)
    bf, f32 = jnp.bfloat16, jnp.float32
    block = padded(feature // n, TILE // 2)
    message = pltpu.VMEM((n, capacity, feature), bf)
    mark = pltpu.VMEM((n, 1, LANES), f32)

    def stages(kind):
        sizes = [feature >> (stage + 1) for stage in range(3)]
        return [
            [pltpu.VMEM((padded(size, TILE // 2), wide), kind) for _, wide in groups]
            for size in sizes
        ]

    return dict(
        tags=pltpu.VMEM((1, tokens), jnp.int32),
        plan=pltpu.VMEM((1, n), jnp.int32),
        helper=pltpu.VMEM((1, tokens), jnp.int32),
        gain=pltpu.VMEM((feature,), f32),
        emb=pltpu.VMEM((tokens, feature), bf),
        cot=pltpu.VMEM((tokens, feature), bf),
        tw=pltpu.VMEM((feature, feature), bf),
        wg=pltpu.VMEM((feature, units), bf),
        wu=pltpu.VMEM((feature, units), bf),
        wd=pltpu.VMEM((units, feature), bf),
        out=[mark, message, message],
        into=[mark, message, message],
        order=pltpu.VMEM((feature, feature), bf),
        hidden=pltpu.VMEM((rows, feature), bf),
        normed=pltpu.VMEM((feature, rows), bf),
        cotan=pltpu.VMEM((rows, feature), bf),
        gate=pltpu.VMEM((rows, units), f32),
        up=pltpu.VMEM((rows, units), f32),
        active=pltpu.VMEM((rows, units), bf),
        d_gate=pltpu.VMEM((rows, units), bf),
        d_up=pltpu.VMEM((rows, units), bf),
        d_rows=pltpu.VMEM((rows, feature), bf),
        held=[
            [pltpu.VMEM((n, hot_slots, wide), bf) for _, wide in column_groups(feature)]
            for _ in (EMB, COT)
        ],
        kept=stages(f32),
        ahead=stages(f32)[0],
        last_kept=[pltpu.VMEM((block, wide), f32) for _, wide in groups],
        last_out=[pltpu.VMEM((1 << (bits - 3), block, wide), bf) for _, wide in groups],
        last_in=[pltpu.VMEM((1 << (bits - 3), block, wide), bf) for _, wide in groups],
        last_send=pltpu.SemaphoreType.DMA((len(groups), 1 << (bits - 3))),
        last_recv=pltpu.SemaphoreType.DMA((len(groups), 1 << (bits - 3))),
        sent=stages(bf),
        came=stages(bf),
        load_sem=pltpu.SemaphoreType.DMA((10,)),
        own_sem=pltpu.SemaphoreType.DMA((3,)),
        send_sem=pltpu.SemaphoreType.DMA((3, n)),
        recv_sem=pltpu.SemaphoreType.DMA((3, n)),
        gather_send=pltpu.SemaphoreType.DMA((2, bits, 3, 4)),
        gather_recv=pltpu.SemaphoreType.DMA((2, bits, 3, 4)),
        reduce_send=pltpu.SemaphoreType.DMA((3, len(groups))),
        reduce_recv=pltpu.SemaphoreType.DMA((3, len(groups))),
    )


def plan_bytes(plan):
    total = 0
    for item in jax.tree.leaves(plan):
        if len(item.shape) > 1 and item.shape[-1] % LANES == 0:
            lead = 1
            for size in item.shape[:-2]:
                lead *= size
            lines = padded(item.shape[-2], TILE // 2)
            total += lead * lines * item.shape[-1] * jnp.dtype(item.dtype).itemsize
    return total


def settle_kernel(count, *refs):
    sems = refs[-1]
    copies = [
        pltpu.make_async_copy(refs[at], refs[count + at], sems.at[at]) for at in range(count)
    ]
    for copy in copies:
        copy.start()
    for copy in copies:
        copy.wait()


def settle(arrays):
    return pl.pallas_call(
        functools.partial(settle_kernel, len(arrays)),
        out_shape=tuple(jax.ShapeDtypeStruct(array.shape, array.dtype) for array in arrays),
        in_specs=[pl.BlockSpec(memory_space=pl.ANY)] * len(arrays),
        out_specs=(pl.BlockSpec(memory_space=pltpu.HBM),) * len(arrays),
        scratch_shapes=[pltpu.SemaphoreType.DMA((len(arrays),))],
        compiler_params=pltpu.CompilerParams(vmem_limit_bytes=1024 * 1024),
    )(*arrays)


def fused_body(embeds, trunk_gain, trunk_weight, w_gate, w_up, w_down, tags, plan, helper, cotangent):
    n = lax.axis_size(("dp", "expert"))
    experts_axis = lax.axis_size("expert")
    tokens, feature = embeds.shape
    units = w_gate.shape[2]
    hot_slots = tokens // 32
    anywhere = pl.BlockSpec(memory_space=pltpu.HBM)
    inside = pl.BlockSpec(memory_space=pltpu.VMEM)
    inputs = dict(
        emb_hbm=(embeds, anywhere),
        gain_hbm=(trunk_gain, anywhere),
        tw_hbm=(trunk_weight, anywhere),
        wg_hbm=(w_gate, anywhere),
        wu_hbm=(w_up, anywhere),
        wd_hbm=(w_down, anywhere),
        tags_hbm=(tags.reshape(1, tokens), anywhere),
        plan_hbm=(plan.reshape(1, -1), anywhere),
        helper_hbm=(helper.reshape(1, tokens), anywhere),
        cot_hbm=(cotangent, anywhere),
    )
    outputs = dict(
        grad_gate=jax.ShapeDtypeStruct(w_gate.shape, jnp.bfloat16),
        grad_up=jax.ShapeDtypeStruct(w_up.shape, jnp.bfloat16),
        grad_down=jax.ShapeDtypeStruct(w_down.shape, jnp.bfloat16),
        grad_trunk=jax.ShapeDtypeStruct((feature // n, feature), jnp.float32),
    )
    scratch = fused_plan(n, hot_slots, tokens, feature, units)
    names = (list(inputs) + list(outputs), jax.tree.structure(scratch))
    results = pl.pallas_call(
        functools.partial(fused_kernel, n, experts_axis, hot_slots, names),
        out_shape=tuple(outputs.values()),
        in_specs=[spec for _, spec in inputs.values()],
        out_specs=(inside,) * len(outputs),
        scratch_shapes=jax.tree.leaves(scratch),
        compiler_params=pltpu.CompilerParams(
            collective_id=0, has_side_effects=True, vmem_limit_bytes=VMEM_BYTES
        ),
    )(*[pltpu.with_memory_space_constraint(value, pltpu.HBM) for value, _ in inputs.values()])
    return settle(results)


def fits(embeds, w_gate, n):
    tokens, feature = embeds.shape
    units = w_gate.shape[2]
    hot_slots = tokens // 32
    if n < 16 or (tokens // n) % 8 or hot_slots % 8 or feature % (16 * n // 4):
        return False
    return plan_bytes(fused_plan(n, hot_slots, tokens, feature, units)) < VMEM_BYTES - 2 * 1024 * 1024


def either(*args):
    n = lax.axis_size(("dp", "expert"))
    return (fused_body if fits(args[0], args[3], n) else body)(*args)


def solution(mesh):
    spread_rows = P(("dp", "expert"), None)
    spread_first = P(("dp", "expert"), None, None)
    return jax.shard_map(
        either,
        mesh=mesh,
        in_specs=(
            spread_rows,
            P(),
            P(),
            spread_first,
            spread_first,
            spread_first,
            P(("dp", "expert")),
            P(),
            P(("dp", "expert")),
            spread_rows,
        ),
        out_specs=(spread_first, spread_first, spread_first, spread_rows),
        check_vma=False,
    )
```
